128 devices in a mesh: gx: 16 (over z, y_hi, core), gy: 8 (over x, y_lo).
Axes of the slice: x: 4, y: 4 (y_hi: 2, y_lo: 2; y = y_hi * 2 + y_lo), z: 4, core: 2. Of those that a mesh axis runs over, the one named last changes fastest.
Arguments:
- latent: bfloat16 [16, 8, 4096, 128], P('gx', 'gy'), may hold values from -6 to 6
- edge_state: bfloat16 [16, 8, 16384, 128], P('gx', 'gy'), may hold values from -6 to 6
- w_first: bfloat16 [384, 128], replicated, may hold values from -0.3125 to 0.3125
- w_second: bfloat16 [128, 128], replicated, may hold values from -0.5 to 0.5
- norm_gain: float32 [128], replicated, may hold values from 0.25 to 1.75
- send_list: int32 [16, 8, 4, 128], P('gx', 'gy'), may hold values from 0 to 4095
- send_count: int32 [16, 8, 4], P('gx', 'gy'), may hold values from 0 to 128, as said below
- halo_list: int32 [16, 8, 4, 1024], P('gx', 'gy'), may hold values from 0 to 4095
- senders: int32 [16, 8, 16384], P('gx', 'gy'), may hold values from 0 to 8703, as said below
- receivers: int32 [16, 8, 16384], P('gx', 'gy'), may hold values from 0 to 4607, as said below
- cotangent_edge: bfloat16 [16, 8, 16384, 128], P('gx', 'gy'), may hold values from -6 to 6
- cotangent_agg: bfloat16 [16, 8, 4608, 128], P('gx', 'gy'), may hold values from -6 to 6
Outputs:
- new_edge: bfloat16 [16, 8, 16384, 128], P('gx', 'gy')
- aggregate: bfloat16 [16, 8, 4608, 128], P('gx', 'gy')
- grad_edge: bfloat16 [16, 8, 16384, 128], P('gx', 'gy')
- grad_latent: float32 [16, 8, 4096, 128], P('gx', 'gy')
- grad_first: float32 [384, 128], replicated
- grad_second: float32 [128, 128], replicated
- grad_gain: float32 [128], replicated
The draws below stay inside these ranges and needn't reach their ends.
Inputs may be any that keep to these rules, and one draw needn't show every extreme that they name: `send_list`: indices into the device's own pre-migration rows. `send_count`: at most 128 particles leave toward one neighbour; some list is full in every draw. `halo_list`: indices into the device's own pre-migration rows. Rows of the device's read table; the 128 edges of each aligned tile have their senders in one aligned block of 128 table rows. Owned rows of the device; the 128 edges of each aligned tile have their receivers in one aligned block of 128 owned rows.
All inputs are finite; a program needn't handle non-finite values.
Results may differ from the reference program's by a relative error of at most 0.0051.
Values may be sent and summed in bfloat16 or wider, within the bound.
A program may use at most 128 MiB of HBM per device.

```python
import jax
import jax.numpy as jnp
from jax import lax

D = 128
HIDDEN_UNITS = 128
TILE = 128
PART_DEV = 4096
MIG_CAP = 128
HALO_ROWS = 1024
EDGE_DEV = 16384
OWNED = 4608
TABLE = 8704
N_GX = 16
N_GY = 8


def draw_send_count(key, part):
    key = jax.random.fold_in(key, 3)
    first_key, second_key = jax.random.split(key)
    counts = jax.random.randint(first_key, (N_GX, N_GY, 4), 0, MIG_CAP + 1)
    chosen = jax.random.randint(second_key, (), 0, N_GX * N_GY * 4)
    flat_index = jnp.arange(N_GX * N_GY * 4, dtype=jnp.int32).reshape(N_GX, N_GY, 4)
    return jnp.where(flat_index == chosen, MIG_CAP, counts).astype(jnp.int32)


def tiled_rows(key, block_count):
    offset_key, row_key, place_key = jax.random.split(key, 3)
    tiles = EDGE_DEV // TILE
    offset = jax.random.randint(offset_key, (N_GX, N_GY, 1), 0, block_count)
    block = (jnp.arange(tiles, dtype=jnp.int32)[None, None, :] + offset) % block_count
    rows = jax.random.randint(row_key, (N_GX, N_GY, tiles, TILE), 0, TILE)
    place = jax.random.randint(place_key, (N_GX, N_GY, tiles, 1), 0, TILE)
    position = jnp.arange(TILE, dtype=jnp.int32)[None, None, None, :]
    rows = jnp.where(position == place, TILE - 1, rows)
    rows = jnp.where(position == (place + 1) % TILE, 0, rows)
    return (block[..., None] * TILE + rows).reshape(N_GX, N_GY, EDGE_DEV).astype(jnp.int32)


def draw_senders(key, part):
    key = jax.random.fold_in(key, 7)
    return tiled_rows(key, TABLE // TILE)


def draw_receivers(key, part):
    key = jax.random.fold_in(key, 11)
    return tiled_rows(key, OWNED // TILE)


def touch_ends(entries, own_key, low, top_value):
    index_at = [jax.random.randint(jax.random.fold_in(own_key, axis), (), 0, length) for axis, length in enumerate(entries.shape)]
    main_axis = entries.shape.index(max(entries.shape))
    beside = index_at[:main_axis] + [(index_at[main_axis] + 1) % entries.shape[main_axis]] + index_at[main_axis + 1:]
    return entries.at[tuple(index_at)].set(low).at[tuple(beside)].set(top_value)


def steps_of(key, dims, cuts, least, top_value):
    level, own = 1.0, jax.random.fold_in(key, 6)
    for dim, blocks in cuts:
        draws = jnp.exp(jax.random.uniform(jax.random.fold_in(own, dim), (blocks,), jnp.float32, least / len(cuts), top_value / len(cuts)))
        level = level * jnp.repeat(draws, dims[dim] // blocks).reshape([-1 if axis == dim else 1 for axis in range(len(dims))])
    return level


def gaussian(key, shape, width, reach, cuts=(), kind=jnp.bfloat16):
    entries = width * jax.random.normal(key, shape, jnp.float32)
    if cuts:
        entries = entries * steps_of(key, shape, cuts, -0.22, 0.18)
    return jnp.clip(entries, -reach, reach).astype(kind)


def setup_inputs(seed: int = 0) -> dict:
    key_list = jax.random.split(jax.random.key(seed), 13)
    return {
        "latent": gaussian(key_list[0], (N_GX, N_GY, PART_DEV, D), 1.0, 6.0, ((0, 16), (1, 8))),
        "edge_state": gaussian(key_list[1], (N_GX, N_GY, EDGE_DEV, D), 1.0, 6.0, ((0, 16), (1, 8))),
        "w_first": gaussian(key_list[2], (3 * D, HIDDEN_UNITS), (3 * D) ** -0.5, 0.3125),
        "w_second": gaussian(key_list[3], (HIDDEN_UNITS, D), HIDDEN_UNITS ** -0.5, 0.5),
        "norm_gain": jnp.clip(1.0 + 0.15 * jax.random.normal(key_list[4], (D,), jnp.float32), 0.25, 1.75),
        "send_list": touch_ends(jax.random.randint(key_list[5], (N_GX, N_GY, 4, MIG_CAP), 0, PART_DEV), jax.random.fold_in(key_list[5], 1), 0, PART_DEV - 1).astype(jnp.int32),
        "send_count": draw_send_count(jax.random.fold_in(key_list[12], 71), 0),
        "halo_list": touch_ends(jax.random.randint(key_list[7], (N_GX, N_GY, 4, HALO_ROWS), 0, PART_DEV), jax.random.fold_in(key_list[7], 1), 0, PART_DEV - 1).astype(jnp.int32),
        "senders": draw_senders(jax.random.fold_in(key_list[12], 71), 0),
        "receivers": draw_receivers(jax.random.fold_in(key_list[12], 71), 0),
        "cotangent_edge": gaussian(key_list[10], (N_GX, N_GY, EDGE_DEV, D), 1.0, 6.0, ((0, 16), (1, 8))),
        "cotangent_agg": gaussian(key_list[11], (N_GX, N_GY, OWNED, D), 1.0, 6.0, ((0, 16), (1, 8))),
    }


eps = 1e-05

def roll_cycle(block, step):
    return jnp.roll(block, step, axis=0)

def shift_wall(block, step):
    zeros = jnp.zeros_like(block[:, :1])
    if step == 1:
        return jnp.concatenate([zeros, block[:, :-1]], axis=1)
    return jnp.concatenate([block[:, 1:], zeros], axis=1)

def arrivals(per_dir):
    return [roll_cycle(per_dir[:, :, 1], 1), roll_cycle(per_dir[:, :, 0], -1), shift_wall(per_dir[:, :, 3], 1), shift_wall(per_dir[:, :, 2], -1)]

def returns(blocks):
    left_x, right_x, left_y, right_y = blocks
    return jnp.stack([roll_cycle(right_x, 1), roll_cycle(left_x, -1), shift_wall(right_y, 1), shift_wall(left_y, -1)], axis=2)

def reference(latent, edge_state, w_first, w_second, norm_gain, send_list, send_count, halo_list, senders, receivers, cotangent_edge, cotangent_agg):
    row_take = jax.vmap(jax.vmap(lambda rows, index: rows[index]))
    slots = jnp.arange(MIG_CAP, dtype=jnp.int32)
    live = slots[None, None, None, :] < send_count[..., None]
    moved = jnp.where(live[..., None], row_take(latent, send_list), jnp.zeros((), jnp.bfloat16)).astype(jnp.bfloat16)
    near = row_take(latent, halo_list)
    table = jnp.concatenate([latent] + arrivals(moved) + arrivals(near), axis=2)
    devices = N_GX * N_GY

    def flat(value):
        return value.reshape((devices,) + value.shape[2:])

    def edge_pass(pack):
        rows, edge, send_idx, recv_idx, cot_edge, cot_agg = pack
        joined = jnp.concatenate([edge, rows[send_idx], rows[recv_idx]], axis=1)
        preact = jnp.dot(joined, w_first, preferred_element_type=jnp.float32)
        hidden = jax.nn.silu(preact).astype(jnp.bfloat16)
        output = jnp.dot(hidden, w_second, preferred_element_type=jnp.float32)
        centred = output - lax.optimization_barrier(jnp.mean(output, axis=-1, keepdims=True))
        inverse = lax.rsqrt(lax.optimization_barrier(jnp.mean(centred * centred, axis=-1, keepdims=True)) + eps)
        normed = centred * inverse
        message = normed * norm_gain
        new_edge = (edge.astype(jnp.float32) + message).astype(jnp.bfloat16)
        aggregate = jax.ops.segment_sum(message, recv_idx, OWNED).astype(jnp.bfloat16)
        d_message = cot_edge.astype(jnp.float32) + cot_agg[recv_idx].astype(jnp.float32)
        d_gain = lax.optimization_barrier(jnp.sum(d_message * normed, axis=0))
        d_norm = d_message * norm_gain
        d_output = (inverse * (d_norm - lax.optimization_barrier(jnp.mean(d_norm, axis=-1, keepdims=True)) - normed * lax.optimization_barrier(jnp.mean(d_norm * normed, axis=-1, keepdims=True)))).astype(jnp.bfloat16)
        d_second = jnp.dot(hidden.T, d_output, preferred_element_type=jnp.float32)
        d_hidden = jnp.dot(d_output, w_second.T, preferred_element_type=jnp.float32)
        sigmoid_v = jax.nn.sigmoid(preact)
        d_preact = (d_hidden * sigmoid_v * (1.0 + preact * (1.0 - sigmoid_v))).astype(jnp.bfloat16)
        d_first = jnp.dot(joined.T, d_preact, preferred_element_type=jnp.float32)
        d_joined = jnp.dot(d_preact, w_first.T, preferred_element_type=jnp.float32)
        grad_edge = (cot_edge.astype(jnp.float32) + d_joined[:, :D]).astype(jnp.bfloat16)
        grad_table = jnp.zeros((TABLE, D), jnp.float32)
        grad_table = grad_table.at[send_idx].add(d_joined[:, D:2 * D]).at[recv_idx].add(d_joined[:, 2 * D:])
        return (new_edge, aggregate, grad_edge, grad_table, d_first, d_second, d_gain)
    results = lax.map(edge_pass, (flat(table), flat(edge_state), flat(senders), flat(receivers), flat(cotangent_edge), flat(cotangent_agg)))
    shape_two = (N_GX, N_GY)
    new_edge = results[0].reshape(shape_two + results[0].shape[1:])
    aggregate = results[1].reshape(shape_two + results[1].shape[1:])
    grad_edge = results[2].reshape(shape_two + results[2].shape[1:])
    grad_table = results[3].reshape(shape_two + results[3].shape[1:])
    grad_first = lax.optimization_barrier(jnp.sum(results[4], axis=0))
    grad_second = lax.optimization_barrier(jnp.sum(results[5], axis=0))
    grad_gain = lax.optimization_barrier(jnp.sum(results[6], axis=0))
    mig_blocks = [grad_table[:, :, PART_DEV + k * MIG_CAP:PART_DEV + (k + 1) * MIG_CAP] for k in range(4)]
    halo_blocks = [grad_table[:, :, OWNED + k * HALO_ROWS:OWNED + (k + 1) * HALO_ROWS] for k in range(4)]
    back_mig = jnp.where(live[..., None], returns(mig_blocks), 0.0)
    back_halo = returns(halo_blocks)

    def scatter_rows(index, values):
        base = jnp.zeros((PART_DEV, D), jnp.float32)
        return base.at[index.reshape(-1)].add(values.reshape(-1, D))
    spread = jax.vmap(jax.vmap(scatter_rows))
    grad_latent = grad_table[:, :, :PART_DEV] + spread(send_list, back_mig) + spread(halo_list, back_halo)
    return (new_edge, aggregate, grad_edge, grad_latent, grad_first, grad_second, grad_gain)
```

```python
import functools

import jax
import jax.numpy as jnp
from jax import lax
from jax.experimental import pallas as pl
from jax.experimental.pallas import tpu as pltpu
from jax.sharding import PartitionSpec as P

MESH = pl.DeviceIdType.MESH
F32 = jnp.float32
BF16 = jnp.bfloat16
TILE = 128
EPS = 1e-05
N_GX = 16
N_GY = 8
OWN_BLOCKS = 32
MIG_BLOCKS = 4
HALO_BLOCKS = 32
OWNED_BLOCKS = OWN_BLOCKS + MIG_BLOCKS
FAR_BLOCKS = MIG_BLOCKS + HALO_BLOCKS
TABLE_BLOCKS = OWN_BLOCKS + FAR_BLOCKS
PER_DIR = HALO_BLOCKS // 4
HALF = OWN_BLOCKS * TILE // 2
PAIRS = 4
RANKS = 32
CHUNK = 24
VMEM_LIMIT = 62 * 2**20
WEIGHT_CHUNK = 16


def mm(a, b):
    return jnp.dot(a, b, preferred_element_type=F32)


def mmt(a, b):
    return lax.dot_general(a, b, (((1,), (1,)), ((), ())), preferred_element_type=F32)


def onehot(rows, row_index, base):
    lanes = row_index.shape[1]
    row = lax.broadcasted_iota(jnp.int16, (rows, lanes), 0)
    index = jnp.broadcast_to((row_index - base).astype(jnp.int16), (rows, lanes))
    return jnp.where(row == index, jnp.ones((), BF16), jnp.zeros((), BF16))


def neighbour(k):
    i = lax.axis_index("gx")
    j = lax.axis_index("gy")
    if k == 0:
        return (lax.rem(i + N_GX - 1, N_GX), j), None
    if k == 1:
        return (lax.rem(i + 1, N_GX), j), None
    if k == 2:
        return (i, j - 1), j > 0
    return (i, j + 1), j < N_GY - 1


def guarded(exists, action):
    if exists is None:
        action()
    else:
        pl.when(exists)(action)


def greet_neighbours(barrier):
    for k in range(4):
        device, exists = neighbour(k)

        def signal(device=device):
            pl.semaphore_signal(barrier, inc=1, device_id=device, device_id_type=MESH)

        guarded(exists, signal)


def neighbour_count():
    j = lax.axis_index("gy")
    return 2 + jnp.where(j > 0, 1, 0) + jnp.where(j < N_GY - 1, 1, 0)


HALO_RUN = 4
RUNS = [(0, 1)] + [(1 + at, HALO_RUN) for at in range(0, PER_DIR, HALO_RUN)]


def table_place(direction, at):
    if at == 0:
        return direction
    return MIG_BLOCKS + direction * PER_DIR + at - 1


def far_copy(src, dst, send_sem, recv_sem, k, run, base, to_slot):
    at, count = RUNS[run]
    device, exists = neighbour(k)
    copy = pltpu.make_async_remote_copy(
        src_ref=src.at[pl.ds(table_place(k, at), count)],
        dst_ref=dst.at[pl.ds(base + table_place(to_slot, at), count)],
        send_sem=send_sem.at[k, run],
        recv_sem=recv_sem.at[to_slot, run],
        device_id=device,
        device_id_type=MESH,
    )
    return copy, exists


def fetch_kernel(
    lat_ref, send_ref, count_ref, halo_ref, snd_ref, rcv_ref,
    tab_ref, meta_ref,
    lat_t, out_buf, zero_buf, send_sem, recv_sem, own_sem, zero_sem,
):
    barrier = pltpu.get_barrier_semaphore()
    greet_neighbours(barrier)

    def turn(b, _):
        rows = lat_ref[pl.ds(pl.multiple_of(b * TILE, TILE), TILE), :]
        lat_t[b] = rows.T
        return 0

    lax.fori_loop(0, OWN_BLOCKS, turn, 0, unroll=4)
    own_copy = pltpu.make_async_copy(lat_t, tab_ref.at[pl.ds(0, OWN_BLOCKS)], own_sem)
    own_copy.start()
    zero_buf[...] = jnp.zeros_like(zero_buf)
    half = OWN_BLOCKS // 2

    def zero_copies(k):
        return [
            pltpu.make_async_copy(
                zero_buf.at[pl.ds(0, count)],
                tab_ref.at[pl.ds(OWN_BLOCKS + table_place(k, at), count)],
                zero_sem.at[k, run],
            )
            for run, (at, count) in enumerate(RUNS)
        ]

    for k in (2, 3):
        _, exists = neighbour(k)

        def fill(k=k):
            for copy in zero_copies(k):
                copy.start()

        pl.when(jnp.logical_not(exists))(fill)

    def pick(index):
        low = jnp.where(index >= HALF, index - HALF, index)
        acc = None
        for piece in range(half // 2):
            hot = onehot(2 * TILE, low, piece * 2 * TILE)
            left = jnp.concatenate(
                [
                    jnp.concatenate([lat_t[2 * piece], lat_t[2 * piece + 1]], axis=1),
                    jnp.concatenate([lat_t[half + 2 * piece], lat_t[half + 2 * piece + 1]], axis=1),
                ],
                axis=0,
            )
            part = mm(left, hot)
            acc = part if acc is None else acc + part
        upper = jnp.broadcast_to(index >= HALF, (TILE, index.shape[1]))
        return jnp.where(upper, acc[TILE:], acc[:TILE]).astype(BF16)

    slot = lax.broadcasted_iota(jnp.int32, (1, TILE), 1)

    def live_index(k):
        return jnp.where(slot < count_ref[k], send_ref[pl.ds(k, 1), :], -1)

    for pair in range(2):
        index = jnp.concatenate([live_index(2 * pair), live_index(2 * pair + 1)], axis=1)
        rows = pick(index)
        out_buf[2 * pair] = rows[:, :TILE]
        out_buf[2 * pair + 1] = rows[:, TILE:]

    pl.semaphore_wait(barrier, neighbour_count())

    def start(k, run):
        copy, exists = far_copy(out_buf, tab_ref, send_sem, recv_sem, k, run, OWN_BLOCKS, k ^ 1)
        guarded(exists, copy.start)

    for k in (2, 3, 0, 1):
        start(k, 0)
    for run in range(1, len(RUNS)):
        at, count = RUNS[run]
        for k in (2, 3, 0, 1):

            def gather(step, _, k=k, at=at):
                first = pl.multiple_of((at - 1) * TILE + step * 2 * TILE, 2 * TILE)
                rows = pick(halo_ref[pl.ds(k, 1), pl.ds(first, 2 * TILE)])
                place = table_place(k, at) + 2 * step
                out_buf[place] = rows[:, :TILE]
                out_buf[place + 1] = rows[:, TILE:]
                return 0

            lax.fori_loop(0, count // 2, gather, 0)
            start(k, run)

    firsts = lax.shift_right_logical(
        jnp.concatenate([snd_ref[...].T[:1], rcv_ref[...].T[:1]], axis=0), 7
    )
    meta_ref[...] = firsts

    own_copy.wait()
    for k in (2, 3):
        _, exists = neighbour(k)

        def drain(k=k):
            for copy in zero_copies(k):
                copy.wait()

        pl.when(jnp.logical_not(exists))(drain)
    for run in range(len(RUNS)):
        for k in range(4):
            copy, exists = far_copy(
                out_buf, tab_ref, send_sem, recv_sem, k, run, OWN_BLOCKS, k ^ 1
            )
            guarded(exists, copy.wait_send)
            back, exists = far_copy(out_buf, tab_ref, send_sem, recv_sem, k, run, OWN_BLOCKS, k)
            guarded(exists, back.wait_recv)


def fetch(nodes, send_rows, counts, halo_rows, send_idx, recv_idx):
    vmem = pl.BlockSpec(memory_space=pltpu.VMEM)
    smem = pl.BlockSpec(memory_space=pltpu.SMEM)
    block = (TILE, TILE)
    return pl.pallas_call(
        fetch_kernel,
        name="fetch_rows",
        out_shape=(
            jax.ShapeDtypeStruct((TABLE_BLOCKS,) + block, BF16),
            jax.ShapeDtypeStruct((2, TILE), jnp.int32),
        ),
        in_specs=[vmem, vmem, smem, vmem, vmem, vmem],
        out_specs=(pl.BlockSpec(memory_space=pl.ANY), vmem),
        scratch_shapes=[
            pltpu.VMEM((OWN_BLOCKS,) + block, BF16),
            pltpu.VMEM((FAR_BLOCKS,) + block, BF16),
            pltpu.VMEM((HALO_RUN,) + block, BF16),
            pltpu.SemaphoreType.DMA((4, len(RUNS))),
            pltpu.SemaphoreType.DMA((4, len(RUNS))),
            pltpu.SemaphoreType.DMA,
            pltpu.SemaphoreType.DMA((4, len(RUNS))),
        ],
        compiler_params=pltpu.CompilerParams(
            collective_id=0, has_side_effects=True, vmem_limit_bytes=VMEM_LIMIT
        ),
        cost_estimate=pl.CostEstimate(
            flops=5 * 10**9, bytes_accessed=8 * 2**20, transcendentals=0
        ),
    )(nodes, send_rows, counts, halo_rows, send_idx, recv_idx)


def edge_kernel(
    meta_ref, edge_ref, cot_ref, snd_ref, rcv_ref, tab_ref, cota_ref,
    w1_ref, w2_ref, gain_ref,
    new_ref, grad_ref, agg_ref, far_ref, own_ref, pay_ref,
    ps_t, pr_t, ca_t, s_acc, ra_acc, fe_acc, w2_acc, g_acc, gain_b, w1_t, w2_t, fsr_acc,
):
    step = pl.program_id(0)
    steps = pl.num_programs(0)

    @pl.when(step == 0)
    def _prologue():
        for part in range(3):
            w1_t[part] = w1_ref[part * TILE : (part + 1) * TILE, :].T
        w2_t[...] = w2_ref[...].T
        gain_b[...] = jnp.broadcast_to(gain_ref[...], (TILE, TILE)).T

        def zero(b, _):
            s_acc[b] = jnp.zeros((TILE, TILE), F32)
            return 0

        lax.fori_loop(0, TABLE_BLOCKS, zero, 0, unroll=2)

        def zero_two(b, _):
            ra_acc[b] = jnp.zeros((TILE, 2 * TILE), F32)
            return 0

        lax.fori_loop(0, OWNED_BLOCKS, zero_two, 0, unroll=2)
        fe_acc[...] = jnp.zeros_like(fe_acc)
        w2_acc[...] = jnp.zeros_like(w2_acc)
        g_acc[...] = jnp.zeros_like(g_acc)

        def project(b, _):
            ps_t[b] = mm(w1_t[1], tab_ref[b]).astype(BF16)
            return 0

        lax.fori_loop(0, TABLE_BLOCKS, project, 0, unroll=4)

        def project_owned(b, _):
            pr_t[b] = mm(w1_t[2], tab_ref[b]).astype(BF16)
            ca_t[b] = cota_ref[pl.ds(pl.multiple_of(b * TILE, TILE), TILE), :].T
            return 0

        lax.fori_loop(0, OWNED_BLOCKS, project_owned, 0, unroll=4)

    we = w1_ref[:TILE, :]
    we_t = w1_t[0]
    w2 = w2_ref[...]
    gain = gain_b[...]
    gain2 = jnp.concatenate([gain, gain], axis=1)

    def pair(p, _):
        tile = (step * PAIRS + p) * 2
        first = pl.multiple_of(p * 2 * TILE, 2 * TILE)
        edges = edge_ref[pl.ds(first, 2 * TILE), :]
        edges_t = edges.T
        cot_t = cot_ref[pl.ds(first, 2 * TILE), :].T.astype(F32)
        hot_s, hot_r, near, cots, blocks = [], [], [], [], []
        for side in range(2):
            bs = meta_ref[0, tile + side]
            br = meta_ref[1, tile + side]
            blocks.append((bs, br))
            hs = onehot(TILE, snd_ref[pl.ds(tile + side, 1), :] & (TILE - 1), 0)
            hr = onehot(TILE, rcv_ref[pl.ds(tile + side, 1), :] & (TILE - 1), 0)
            hot_s.append(hs)
            hot_r.append(hr)
            near.append(
                mm(
                    jnp.concatenate([ps_t[bs], pr_t[br]], axis=1),
                    jnp.concatenate([hs, hr], axis=0),
                )
            )
            cots.append(mm(ca_t[br], hr))
        preact = mm(we_t, edges_t) + jnp.concatenate(near, axis=1)
        sig = 0.5 * jnp.tanh(0.5 * preact) + 0.5
        hidden = preact * sig
        slope = sig + hidden * (1.0 - sig)
        hidden = hidden.astype(BF16)
        output = mm(w2_t[...], hidden)
        centred = output - jnp.sum(output, axis=0, keepdims=True) * (1.0 / TILE)
        variance = jnp.sum(centred * centred, axis=0, keepdims=True) * (1.0 / TILE)
        inverse = lax.rsqrt(variance + EPS)
        normed = centred * inverse
        message = normed * gain2
        new_edge = (edges_t.astype(F32) + message).astype(BF16)
        new_ref[pl.ds(first, 2 * TILE), :] = new_edge.T
        message = message.astype(BF16)
        d_message = cot_t + jnp.concatenate(cots, axis=1)
        weighted = d_message * normed
        g_acc[...] += weighted
        d_norm = d_message * gain2
        mean_one = jnp.sum(d_norm, axis=0, keepdims=True) * (1.0 / TILE)
        mean_two = jnp.sum(weighted * gain2, axis=0, keepdims=True) * (1.0 / TILE)
        d_output = (inverse * (d_norm - mean_one - normed * mean_two)).astype(BF16)
        w2_acc[...] += mmt(hidden, d_output)
        d_preact = (mm(w2, d_output) * slope).astype(BF16)
        fe_acc[...] += mm(d_preact, edges)
        grad_edge = (cot_t + mm(we, d_preact)).astype(BF16)
        grad_ref[pl.ds(first, 2 * TILE), :] = grad_edge.T
        for side in range(2):
            bs, br = blocks[side]
            lanes = slice(side * TILE, (side + 1) * TILE)
            d_pre = d_preact[:, lanes]
            s_acc[bs] += mmt(hot_s[side], d_pre)
            both = jnp.concatenate([d_pre, message[:, lanes]], axis=0)
            ra_acc[br] += mmt(hot_r[side], both)
        return 0

    lax.fori_loop(0, PAIRS, pair, 0, unroll=2)

    @pl.when(step == steps - 1)
    def _epilogue():
        ws = w1_ref[TILE : 2 * TILE, :]
        wr = w1_ref[2 * TILE :, :]
        wsr = jnp.concatenate([ws, wr], axis=1)

        fsr_acc[...] = jnp.zeros_like(fsr_acc)

        def own(b, _):
            s = s_acc[b].astype(BF16)
            ra = ra_acc[b]
            r = ra[:, :TILE].astype(BF16)
            rows = pl.ds(pl.multiple_of(b * TILE, TILE), TILE)
            agg_ref[rows, :] = ra[:, TILE:].astype(BF16)
            both = jnp.concatenate([s, r], axis=1)
            own_ref[rows, :] = mmt(both, wsr)
            fsr_acc[...] += mm(tab_ref[b], both)
            return 0

        lax.fori_loop(0, OWN_BLOCKS, own, 0, unroll=4)

        def migrated(b, _):
            s = s_acc[b].astype(BF16)
            ra = ra_acc[b]
            r = ra[:, :TILE].astype(BF16)
            rows = pl.ds(pl.multiple_of(b * TILE, TILE), TILE)
            agg_ref[rows, :] = ra[:, TILE:].astype(BF16)
            both = jnp.concatenate([s, r], axis=1)
            far_ref[b - OWN_BLOCKS] = mmt(wsr, both).astype(BF16)
            fsr_acc[...] += mm(tab_ref[b], both)
            return 0

        lax.fori_loop(OWN_BLOCKS, OWNED_BLOCKS, migrated, 0, unroll=4)

        def halo(b, _):
            s = s_acc[b].astype(BF16)
            far_ref[b - OWN_BLOCKS] = mmt(ws, s).astype(BF16)
            fsr_acc[:, :TILE] += mm(tab_ref[b], s)
            return 0

        lax.fori_loop(OWNED_BLOCKS, TABLE_BLOCKS, halo, 0, unroll=4)
        first = fsr_acc[:, :TILE]
        second = fsr_acc[:, TILE:]
        edge_part = fe_acc[...].T
        w2_part = w2_acc[...]
        g_part = g_acc[:, :TILE] + g_acc[:, TILE:]
        g_row = jnp.sum(g_part.T, axis=0, keepdims=True)
        g_tile = jnp.broadcast_to(g_row, (CHUNK - WEIGHT_CHUNK, TILE))
        per = TILE // WEIGHT_CHUNK
        for n, part in enumerate((edge_part, first, second, w2_part)):
            for c in range(per):
                pay_ref[n * per + c, :WEIGHT_CHUNK, :] = part[
                    c * WEIGHT_CHUNK : (c + 1) * WEIGHT_CHUNK
                ]
                pay_ref[n * per + c, WEIGHT_CHUNK:, :] = g_tile


def edge_pass(meta, edges, cot_edge, send_idx, recv_idx, table, cot_agg, w_first, w_second, gain):
    rows = PAIRS * 2 * TILE
    steps = edges.shape[0] // rows
    block = (TILE, TILE)

    def whole(*shape):
        return pl.BlockSpec(shape, lambda s, m: (0,) * len(shape))

    stream = pl.BlockSpec((rows, TILE), lambda s, m: (s, 0))
    return pl.pallas_call(
        edge_kernel,
        name="edge_block",
        grid_spec=pltpu.PrefetchScalarGridSpec(
            num_scalar_prefetch=1,
            grid=(steps,),
            in_specs=[
                stream,
                stream,
                whole(*send_idx.shape),
                whole(*recv_idx.shape),
                whole(*table.shape),
                whole(*cot_agg.shape),
                whole(*w_first.shape),
                whole(*w_second.shape),
                whole(*gain.shape),
            ],
            out_specs=[
                stream,
                stream,
                whole(OWNED_BLOCKS * TILE, TILE),
                whole(FAR_BLOCKS, TILE, TILE),
                whole(OWN_BLOCKS * TILE, TILE),
                whole(RANKS, CHUNK, TILE),
            ],
            scratch_shapes=[
                pltpu.VMEM((TABLE_BLOCKS,) + block, BF16),
                pltpu.VMEM((OWNED_BLOCKS,) + block, BF16),
                pltpu.VMEM((OWNED_BLOCKS,) + block, BF16),
                pltpu.VMEM((TABLE_BLOCKS,) + block, F32),
                pltpu.VMEM((OWNED_BLOCKS, TILE, 2 * TILE), F32),
                pltpu.VMEM(block, F32),
                pltpu.VMEM(block, F32),
                pltpu.VMEM((TILE, 2 * TILE), F32),
                pltpu.VMEM(block, F32),
                pltpu.VMEM((3,) + block, BF16),
                pltpu.VMEM(block, BF16),
                pltpu.VMEM((TILE, 2 * TILE), F32),
            ],
        ),
        out_shape=[
            jax.ShapeDtypeStruct(edges.shape, BF16),
            jax.ShapeDtypeStruct(edges.shape, BF16),
            jax.ShapeDtypeStruct((OWNED_BLOCKS * TILE, TILE), BF16),
            jax.ShapeDtypeStruct((FAR_BLOCKS, TILE, TILE), BF16),
            jax.ShapeDtypeStruct((OWN_BLOCKS * TILE, TILE), F32),
            jax.ShapeDtypeStruct((RANKS, CHUNK, TILE), F32),
        ],
        compiler_params=pltpu.CompilerParams(vmem_limit_bytes=VMEM_LIMIT),
        cost_estimate=pl.CostEstimate(
            flops=12 * 10**9, bytes_accessed=24 * 2**20, transcendentals=3 * 2**20
        ),
    )(meta, edges, cot_edge, send_idx, recv_idx, table, cot_agg, w_first, w_second, gain)


def rank_device(rank):
    i = lax.axis_index("gx")
    j = lax.axis_index("gy")
    gx = (rank // 8) * 4 + (lax.rem(i, 4) // 2) * 2 + lax.rem(rank, 2)
    gy = lax.rem(rank // 2, 4) * 2 + lax.rem(j, 2)
    return gx, gy


def my_rank():
    i = lax.axis_index("gx")
    j = lax.axis_index("gy")
    return (i // 4) * 8 + (j // 2) * 2 + lax.rem(i, 2)


def column_device(place):
    i = lax.axis_index("gx")
    j = lax.axis_index("gy")
    return (i // 4) * 4 + (place // 2) * 2 + lax.rem(i, 2), (j // 2) * 2 + lax.rem(place, 2)


def my_place():
    i = lax.axis_index("gx")
    j = lax.axis_index("gy")
    return (lax.rem(i, 4) // 2) * 2 + lax.rem(j, 2)


def return_kernel(
    far_ref, own_ref, pay_ref, send_ref, count_ref, halo_ref,
    lat_ref, sum_ref,
    back, mine, ring, col, acc, got,
    send_sem, recv_sem, rs_send, rs_recv, col_send, col_recv, ag_send, ag_recv,
):
    rank = my_rank()
    place = my_place()
    barrier = pltpu.get_barrier_semaphore()
    greet_neighbours(barrier)

    def greet(s, _):
        device = rank_device(lax.rem(rank + s, RANKS))
        pl.semaphore_signal(barrier, inc=1, device_id=device, device_id_type=MESH)
        return 0

    lax.fori_loop(1, RANKS, greet, 0)
    for s in range(1, 4):
        device = column_device(lax.rem(place + s, 4))
        pl.semaphore_signal(barrier, inc=1, device_id=device, device_id_type=MESH)

    acc[:, :TILE] = own_ref[:HALF, :]
    acc[:, TILE:] = own_ref[HALF:, :]
    pl.semaphore_wait(barrier, neighbour_count() + RANKS - 1 + 3)

    def give(k, run, to_slot):
        return far_copy(far_ref, back, send_sem, recv_sem, k, run, 0, to_slot)

    for run in range(len(RUNS)):
        for k in (2, 3, 0, 1):
            copy, exists = give(k, run, k ^ 1)
            guarded(exists, copy.start)

    def scatter_copy(s):
        to = lax.rem(rank + s, RANKS)
        return pltpu.make_async_remote_copy(
            src_ref=pay_ref.at[to],
            dst_ref=ring.at[rank],
            send_sem=rs_send.at[s],
            recv_sem=rs_recv.at[s],
            device_id=rank_device(to),
            device_id_type=MESH,
        )

    def start_scatter(s, _):
        scatter_copy(s).start()
        return 0

    lax.fori_loop(1, RANKS, start_scatter, 0)

    def wait_scatter(s, _):
        scatter_copy(s).wait()
        return 0

    lax.fori_loop(1, RANKS, wait_scatter, 0)

    ring[rank] = pay_ref[rank]

    def add_up(s, total):
        return total + ring[s]

    col[0] = lax.fori_loop(1, RANKS, add_up, ring[0], unroll=8)

    def column_copy(s):
        return pltpu.make_async_remote_copy(
            src_ref=col.at[0],
            dst_ref=col.at[s],
            send_sem=col_send.at[s],
            recv_sem=col_recv.at[s],
            device_id=column_device(lax.rem(place + s, 4)),
            device_id_type=MESH,
        )

    for s in range(1, 4):
        column_copy(s).start()

    slot = lax.broadcasted_iota(jnp.int32, (1, TILE), 1)

    def spread(index, values_t):
        upper = jnp.broadcast_to(index >= HALF, values_t.shape)
        none = jnp.zeros((), BF16)
        right = jnp.concatenate(
            [jnp.where(upper, none, values_t), jnp.where(upper, values_t, none)], axis=0
        )
        low = jnp.where(index >= HALF, index - HALF, index)

        def piece(m, _):
            first = pl.multiple_of(m * 2 * TILE, 2 * TILE)
            hot = onehot(2 * TILE, low, first)
            acc[pl.ds(first, 2 * TILE), :] += mmt(hot, right)
            return 0

        lax.fori_loop(0, HALF // (2 * TILE), piece, 0)

    for k in range(4):
        copy, exists = give(k, 0, k)
        guarded(exists, copy.wait_recv)
        copy, exists = give(k, 0, k ^ 1)
        guarded(exists, copy.wait_send)
    indices, values = [], []
    for k in range(4):
        _, exists = neighbour(k)
        live = slot < count_ref[k]
        if exists is not None:
            live = jnp.logical_and(live, exists)
        indices.append(jnp.where(live, send_ref[pl.ds(k, 1), :], -1))
        blockv = back[k]
        if exists is not None:
            blockv = jnp.where(jnp.broadcast_to(live, (TILE, TILE)), blockv, jnp.zeros((), BF16))
        values.append(blockv)
    spread(jnp.concatenate(indices, axis=1), jnp.concatenate(values, axis=1))

    for s in range(1, 4):
        column_copy(s).wait()
    total = (col[0] + col[2]) + (col[1] + col[3])
    mine[...] = total[:WEIGHT_CHUNK]
    got[rank] = total[:WEIGHT_CHUNK]
    sum_ref[pl.ds(RANKS * WEIGHT_CHUNK, CHUNK - WEIGHT_CHUNK), :] = total[WEIGHT_CHUNK:]

    def gather_copy(s, owner):
        return pltpu.make_async_remote_copy(
            src_ref=mine,
            dst_ref=got.at[owner],
            send_sem=ag_send.at[s],
            recv_sem=ag_recv.at[s],
            device_id=rank_device(lax.rem(rank + s, RANKS)),
            device_id_type=MESH,
        )

    def start_gather(s, _):
        gather_copy(s, rank).start()
        return 0

    lax.fori_loop(1, RANKS, start_gather, 0)

    for run in range(1, len(RUNS)):
        at, count = RUNS[run]
        for k in (0, 1, 2, 3):
            copy, exists = give(k, run, k)

            def take(copy=copy, k=k, at=at, count=count):
                copy.wait_recv()
                first = table_place(k, at)
                index = halo_ref[pl.ds(k, 1), pl.ds((at - 1) * TILE, count * TILE)]
                spread(index, jnp.concatenate([back[first + n] for n in range(count)], axis=1))

            guarded(exists, take)
    for run in range(1, len(RUNS)):
        for k in range(4):
            copy, exists = give(k, run, k ^ 1)
            guarded(exists, copy.wait_send)

    def wait_gather(s, _):
        owner = lax.rem(rank + RANKS - s, RANKS)
        gather_copy(s, owner).wait()
        return 0

    lax.fori_loop(1, RANKS, wait_gather, 0)
    for c in range(RANKS):
        sum_ref[c * WEIGHT_CHUNK : (c + 1) * WEIGHT_CHUNK, :] = got[c]
    lat_ref[:HALF, :] = acc[:, :TILE]
    lat_ref[HALF:, :] = acc[:, TILE:]


def give_back(far, own, payload, send_rows, counts, halo_rows):
    vmem = pl.BlockSpec(memory_space=pltpu.VMEM)
    smem = pl.BlockSpec(memory_space=pltpu.SMEM)
    dma = pltpu.SemaphoreType.DMA
    return pl.pallas_call(
        return_kernel,
        name="return_rows",
        out_shape=(
            jax.ShapeDtypeStruct((OWN_BLOCKS * TILE, TILE), F32),
            jax.ShapeDtypeStruct((RANKS * WEIGHT_CHUNK + CHUNK - WEIGHT_CHUNK, TILE), F32),
        ),
        in_specs=[vmem, vmem, vmem, vmem, smem, vmem],
        out_specs=(vmem, vmem),
        scratch_shapes=[
            pltpu.VMEM((FAR_BLOCKS, TILE, TILE), BF16),
            pltpu.VMEM((WEIGHT_CHUNK, TILE), F32),
            pltpu.VMEM((RANKS, CHUNK, TILE), F32),
            pltpu.VMEM((4, CHUNK, TILE), F32),
            pltpu.VMEM((HALF, 2 * TILE), F32),
            pltpu.VMEM((RANKS, WEIGHT_CHUNK, TILE), F32),
            dma((4, len(RUNS))),
            dma((4, len(RUNS))),
            dma((RANKS,)),
            dma((RANKS,)),
            dma((4,)),
            dma((4,)),
            dma((RANKS,)),
            dma((RANKS,)),
        ],
        compiler_params=pltpu.CompilerParams(
            collective_id=1, has_side_effects=True, vmem_limit_bytes=VMEM_LIMIT
        ),
        cost_estimate=pl.CostEstimate(
            flops=5 * 10**9, bytes_accessed=8 * 2**20, transcendentals=0
        ),
    )(far, own, payload, send_rows, counts, halo_rows)


def per_device(
    latent,
    edge_state,
    w_first,
    w_second,
    norm_gain,
    send_list,
    send_count,
    halo_list,
    senders,
    receivers,
    cotangent_edge,
    cotangent_agg,
):
    send_rows = send_list[0, 0]
    halo_rows = halo_list[0, 0]
    counts = send_count[0, 0]
    send_idx = senders.reshape(-1, TILE)
    recv_idx = receivers.reshape(-1, TILE)
    table, meta = fetch(latent[0, 0], send_rows, counts, halo_rows, send_idx, recv_idx)
    new_edge, grad_edge, aggregate, far, own, payload = edge_pass(
        meta,
        edge_state[0, 0],
        cotangent_edge[0, 0],
        send_idx,
        recv_idx,
        table,
        cotangent_agg[0, 0],
        w_first,
        w_second,
        norm_gain.reshape(1, TILE),
    )
    grad_latent, sums = give_back(far, own, payload, send_rows, counts, halo_rows)
    return (
        new_edge[None, None],
        aggregate[None, None],
        grad_edge[None, None],
        grad_latent[None, None],
        sums[: 3 * TILE],
        sums[3 * TILE : 4 * TILE],
        sums[4 * TILE],
    )


def solution(mesh):
    rows = P("gx", "gy", None, None)
    flat = P("gx", "gy", None)
    in_specs = (rows, rows, P(), P(), P(), rows, flat, rows, flat, flat, rows, rows)
    out_specs = (rows, rows, rows, rows, P(), P(), P())
    return jax.shard_map(
        per_device, mesh=mesh, in_specs=in_specs, out_specs=out_specs, check_vma=False
    )
```

```python
import functools

import jax
import jax.numpy as jnp
from jax import lax
from jax.experimental import pallas as pl
from jax.experimental.pallas import tpu as pltpu
from jax.sharding import PartitionSpec as P

MESH = pl.DeviceIdType.MESH
F32 = jnp.float32
BF16 = jnp.bfloat16
TILE = 128
EPS = 1e-05
N_GX = 16
N_GY = 8
OWN_BLOCKS = 32
MIG_BLOCKS = 4
HALO_BLOCKS = 32
OWNED_BLOCKS = OWN_BLOCKS + MIG_BLOCKS
FAR_BLOCKS = MIG_BLOCKS + HALO_BLOCKS
TABLE_BLOCKS = OWN_BLOCKS + FAR_BLOCKS
PER_DIR = HALO_BLOCKS // 4
HALF = OWN_BLOCKS * TILE // 2
GROUP = 16
GROUPS = 1
UNROLL = 1
RANKS = 32
CHUNK = 24
VMEM_LIMIT = 62 * 2**20
RETURN_LIMIT = 24 * 2**20
WEIGHT_CHUNK = 16


def mm(a, b):
    return jnp.dot(a, b, preferred_element_type=F32)


def mmt(a, b):
    return lax.dot_general(a, b, (((1,), (1,)), ((), ())), preferred_element_type=F32)


def onehot(rows, row_index, base):
    lanes = row_index.shape[1]
    row = lax.broadcasted_iota(jnp.int16, (rows, lanes), 0)
    index = jnp.broadcast_to((row_index - base).astype(jnp.int16), (rows, lanes))
    return jnp.where(row == index, jnp.ones((), BF16), jnp.zeros((), BF16))


def neighbour(k):
    i = lax.axis_index("gx")
    j = lax.axis_index("gy")
    if k == 0:
        return (lax.rem(i + N_GX - 1, N_GX), j), None
    if k == 1:
        return (lax.rem(i + 1, N_GX), j), None
    if k == 2:
        return (i, j - 1), j > 0
    return (i, j + 1), j < N_GY - 1


def guarded(exists, action):
    if exists is None:
        action()
    else:
        pl.when(exists)(action)


def greet_neighbours(barrier):
    for k in range(4):
        device, exists = neighbour(k)

        def signal(device=device):
            pl.semaphore_signal(barrier, inc=1, device_id=device, device_id_type=MESH)

        guarded(exists, signal)


def neighbour_count():
    j = lax.axis_index("gy")
    return 2 + jnp.where(j > 0, 1, 0) + jnp.where(j < N_GY - 1, 1, 0)


X_RUNS = ((0, 1), (1, 4), (5, 4))
Y_RUNS = ((0, 1), (1, 4), (5, 2), (7, 2))
RUNS = (X_RUNS, X_RUNS, Y_RUNS, Y_RUNS)
MOST_RUNS = 4
LONGEST = 4
ORDER = (
    [(k, 0) for k in (2, 3, 0, 1)]
    + [(k, run) for run in (1, 2) for k in (0, 1)]
    + [(k, run) for run in (1, 2, 3) for k in (2, 3)]
)
X_END = 4 + 4


def table_place(direction, at):
    if at == 0:
        return direction
    return MIG_BLOCKS + direction * PER_DIR + at - 1


def far_copy(src, dst, send_sem, recv_sem, k, run, base, to_slot):
    at, count = RUNS[k][run]
    device, exists = neighbour(k)
    copy = pltpu.make_async_remote_copy(
        src_ref=src.at[pl.ds(table_place(k, at), count)],
        dst_ref=dst.at[pl.ds(base + table_place(to_slot, at), count)],
        send_sem=send_sem.at[k, run],
        recv_sem=recv_sem.at[to_slot, run],
        device_id=device,
        device_id_type=MESH,
    )
    return copy, exists


def fetch_kernel(
    lat_ref, send_ref, count_ref, halo_ref, snd_ref, rcv_ref,
    tab_ref, meta_ref,
    lat_t, out_buf, zero_buf, send_sem, recv_sem, own_sem, zero_sem,
):
    barrier = pltpu.get_barrier_semaphore()
    greet_neighbours(barrier)

    def turn(b, _):
        rows = lat_ref[pl.ds(pl.multiple_of(b * TILE, TILE), TILE), :]
        lat_t[b] = rows.T
        return 0

    lax.fori_loop(0, OWN_BLOCKS, turn, 0, unroll=4)
    own_copy = pltpu.make_async_copy(lat_t, tab_ref.at[pl.ds(0, OWN_BLOCKS)], own_sem)
    own_copy.start()
    zero_buf[...] = jnp.zeros_like(zero_buf)
    half = OWN_BLOCKS // 2

    def zero_copies(k):
        return [
            pltpu.make_async_copy(
                zero_buf.at[pl.ds(0, count)],
                tab_ref.at[pl.ds(OWN_BLOCKS + table_place(k, at), count)],
                zero_sem.at[k, run],
            )
            for run, (at, count) in enumerate(RUNS[k])
        ]

    for k in (2, 3):
        _, exists = neighbour(k)

        def fill(k=k):
            for copy in zero_copies(k):
                copy.start()

        pl.when(jnp.logical_not(exists))(fill)

    def pick(index):
        low = jnp.where(index >= HALF, index - HALF, index)
        acc = None
        for piece in range(half // 2):
            hot = onehot(2 * TILE, low, piece * 2 * TILE)
            left = jnp.concatenate(
                [
                    jnp.concatenate([lat_t[2 * piece], lat_t[2 * piece + 1]], axis=1),
                    jnp.concatenate([lat_t[half + 2 * piece], lat_t[half + 2 * piece + 1]], axis=1),
                ],
                axis=0,
            )
            part = mm(left, hot)
            acc = part if acc is None else acc + part
        upper = jnp.broadcast_to(index >= HALF, (TILE, index.shape[1]))
        return jnp.where(upper, acc[TILE:], acc[:TILE]).astype(BF16)

    slot = lax.broadcasted_iota(jnp.int32, (1, TILE), 1)

    def live_index(k):
        return jnp.where(slot < count_ref[k], send_ref[pl.ds(k, 1), :], -1)

    for pair in range(2):
        index = jnp.concatenate([live_index(2 * pair), live_index(2 * pair + 1)], axis=1)
        rows = pick(index)
        out_buf[2 * pair] = rows[:, :TILE]
        out_buf[2 * pair + 1] = rows[:, TILE:]

    pl.semaphore_wait(barrier, neighbour_count())

    def start(k, run):
        copy, exists = far_copy(out_buf, tab_ref, send_sem, recv_sem, k, run, OWN_BLOCKS, k ^ 1)
        guarded(exists, copy.start)

    for k, run in ORDER:
        at, count = RUNS[k][run]
        if at:

            def gather(step, _, k=k, at=at):
                first = pl.multiple_of((at - 1) * TILE + step * 2 * TILE, 2 * TILE)
                rows = pick(halo_ref[pl.ds(k, 1), pl.ds(first, 2 * TILE)])
                place = table_place(k, at) + 2 * step
                out_buf[place] = rows[:, :TILE]
                out_buf[place + 1] = rows[:, TILE:]
                return 0

            lax.fori_loop(0, count // 2, gather, 0)
        start(k, run)

    firsts = lax.shift_right_logical(
        jnp.concatenate([snd_ref[...].T[:1], rcv_ref[...].T[:1]], axis=0), 7
    )
    meta_ref[...] = firsts

    own_copy.wait()
    for k in (2, 3):
        _, exists = neighbour(k)

        def drain(k=k):
            for copy in zero_copies(k):
                copy.wait()

        pl.when(jnp.logical_not(exists))(drain)
    for k, run in ORDER:
        copy, exists = far_copy(out_buf, tab_ref, send_sem, recv_sem, k, run, OWN_BLOCKS, k ^ 1)
        guarded(exists, copy.wait_send)
        back, exists = far_copy(out_buf, tab_ref, send_sem, recv_sem, k, run, OWN_BLOCKS, k)
        guarded(exists, back.wait_recv)


def fetch(nodes, send_rows, counts, halo_rows, send_idx, recv_idx):
    vmem = pl.BlockSpec(memory_space=pltpu.VMEM)
    smem = pl.BlockSpec(memory_space=pltpu.SMEM)
    block = (TILE, TILE)
    return pl.pallas_call(
        fetch_kernel,
        name="fetch_rows",
        out_shape=(
            jax.ShapeDtypeStruct((TABLE_BLOCKS,) + block, BF16),
            jax.ShapeDtypeStruct((2, TILE), jnp.int32),
        ),
        in_specs=[vmem, vmem, smem, vmem, vmem, vmem],
        out_specs=(pl.BlockSpec(memory_space=pl.ANY), vmem),
        scratch_shapes=[
            pltpu.VMEM((OWN_BLOCKS,) + block, BF16),
            pltpu.VMEM((FAR_BLOCKS,) + block, BF16),
            pltpu.VMEM((LONGEST,) + block, BF16),
            pltpu.SemaphoreType.DMA((4, MOST_RUNS)),
            pltpu.SemaphoreType.DMA((4, MOST_RUNS)),
            pltpu.SemaphoreType.DMA,
            pltpu.SemaphoreType.DMA((4, MOST_RUNS)),
        ],
        compiler_params=pltpu.CompilerParams(
            collective_id=0, has_side_effects=True, vmem_limit_bytes=VMEM_LIMIT
        ),
        cost_estimate=pl.CostEstimate(
            flops=5 * 10**9, bytes_accessed=8 * 2**20, transcendentals=0
        ),
    )(nodes, send_rows, counts, halo_rows, send_idx, recv_idx)


def edge_kernel(
    meta_ref, edge_ref, cot_ref, snd_ref, rcv_ref, tab_ref, cota_ref,
    w1_ref, w2_ref, gain_ref,
    new_ref, grad_ref, agg_ref, far_ref, own_ref, pay_ref,
    ps_t, pr_t, ca_t, s_acc, ra_acc, fe_acc, w2_acc, g_acc, gain_b, w1_t, w2_t, fsr_acc,
):
    step = pl.program_id(0)
    steps = pl.num_programs(0)

    @pl.when(step == 0)
    def _prologue():
        for part in range(3):
            w1_t[part] = w1_ref[part * TILE : (part + 1) * TILE, :].T
        w2_t[...] = w2_ref[...].T
        gain_b[...] = jnp.broadcast_to(gain_ref[...], (TILE, TILE)).T

        def zero(b, _):
            s_acc[b] = jnp.zeros((TILE, TILE), F32)
            return 0

        lax.fori_loop(0, TABLE_BLOCKS, zero, 0, unroll=2)

        def zero_two(b, _):
            ra_acc[b] = jnp.zeros((TILE, 2 * TILE), F32)
            return 0

        lax.fori_loop(0, OWNED_BLOCKS, zero_two, 0, unroll=2)
        fe_acc[...] = jnp.zeros_like(fe_acc)
        w2_acc[...] = jnp.zeros_like(w2_acc)
        g_acc[...] = jnp.zeros_like(g_acc)

        def project(at, _):
            first = at * 4
            blocks = jnp.concatenate([tab_ref[first + n] for n in range(4)], axis=1)
            out = mm(w1_t[1], blocks).astype(BF16)
            for n in range(4):
                ps_t[first + n] = out[:, n * TILE : (n + 1) * TILE]
            return 0

        lax.fori_loop(0, TABLE_BLOCKS // 4, project, 0)

        def project_owned(at, _):
            first = at * 4
            blocks = jnp.concatenate([tab_ref[first + n] for n in range(4)], axis=1)
            out = mm(w1_t[2], blocks).astype(BF16)
            rows = pl.ds(pl.multiple_of(first * TILE, 4 * TILE), 4 * TILE)
            turned = cota_ref[rows, :].T
            for n in range(4):
                pr_t[first + n] = out[:, n * TILE : (n + 1) * TILE]
                ca_t[first + n] = turned[:, n * TILE : (n + 1) * TILE]
            return 0

        lax.fori_loop(0, OWNED_BLOCKS // 4, project_owned, 0)

    we = w1_ref[:TILE, :]
    we_t = w1_t[0]
    w2 = w2_ref[...]
    gain = jnp.concatenate([gain_b[...]] * GROUP, axis=1)
    wide = GROUP * TILE

    def group(p, _):
        tile = (step * GROUPS + p) * GROUP
        first = pl.multiple_of(p * wide, wide)
        rows = pl.ds(first, wide)
        edges = edge_ref[rows, :]
        edges_t = edges.T
        cot_t = cot_ref[rows, :].T.astype(F32)
        hot_s, hot_r, near, cots, blocks = [], [], [], [], []
        for side in range(GROUP):
            bs = meta_ref[0, tile + side]
            br = meta_ref[1, tile + side]
            blocks.append((bs, br))
            hs = onehot(TILE, snd_ref[pl.ds(tile + side, 1), :] & (TILE - 1), 0)
            hr = onehot(TILE, rcv_ref[pl.ds(tile + side, 1), :] & (TILE - 1), 0)
            hot_s.append(hs)
            hot_r.append(hr)
            near.append(
                mm(
                    jnp.concatenate([ps_t[bs], pr_t[br]], axis=1),
                    jnp.concatenate([hs, hr], axis=0),
                )
            )
            cots.append(mm(ca_t[br], hr))
        preact = mm(we_t, edges_t) + jnp.concatenate(near, axis=1)
        sig = 0.5 * jnp.tanh(0.5 * preact) + 0.5
        hidden = preact * sig
        slope = sig + hidden * (1.0 - sig)
        hidden = hidden.astype(BF16)
        output = mm(w2_t[...], hidden)
        centred = output - jnp.sum(output, axis=0, keepdims=True) * (1.0 / TILE)
        variance = jnp.sum(centred * centred, axis=0, keepdims=True) * (1.0 / TILE)
        inverse = lax.rsqrt(variance + EPS)
        normed = centred * inverse
        message = normed * gain
        new_edge = (edges_t.astype(F32) + message).astype(BF16)
        new_ref[rows, :] = new_edge.T
        message = message.astype(BF16)
        d_message = cot_t + jnp.concatenate(cots, axis=1)
        weighted = d_message * normed
        g_sum = weighted[:, :TILE]
        for side in range(1, GROUP):
            g_sum += weighted[:, side * TILE : (side + 1) * TILE]
        g_acc[...] += g_sum
        d_norm = d_message * gain
        mean_one = jnp.sum(d_norm, axis=0, keepdims=True) * (1.0 / TILE)
        mean_two = jnp.sum(weighted * gain, axis=0, keepdims=True) * (1.0 / TILE)
        d_output = (inverse * (d_norm - mean_one - normed * mean_two)).astype(BF16)
        w2_acc[...] += mmt(hidden, d_output)
        d_preact = (mm(w2, d_output) * slope).astype(BF16)
        fe_acc[...] += mm(d_preact, edges)
        grad_edge = (cot_t + mm(we, d_preact)).astype(BF16)
        grad_ref[rows, :] = grad_edge.T
        for side in range(GROUP):
            bs, br = blocks[side]
            lanes = slice(side * TILE, (side + 1) * TILE)
            d_pre = d_preact[:, lanes]
            s_acc[bs] += mmt(hot_s[side], d_pre)
            both = jnp.concatenate([d_pre, message[:, lanes]], axis=0)
            ra_acc[br] += mmt(hot_r[side], both)
        return 0

    lax.fori_loop(0, GROUPS, group, 0, unroll=UNROLL)

    @pl.when(step == steps - 1)
    def _epilogue():
        ws = w1_ref[TILE : 2 * TILE, :]
        wr = w1_ref[2 * TILE :, :]
        wsr = jnp.concatenate([ws, wr], axis=1)

        fsr_acc[...] = jnp.zeros_like(fsr_acc)

        def owned(at):
            first = at * 4
            rows = pl.ds(pl.multiple_of(first * TILE, 4 * TILE), 4 * TILE)
            s = jnp.concatenate([s_acc[first + n].astype(BF16) for n in range(4)], axis=0)
            ra = [ra_acc[first + n] for n in range(4)]
            r = jnp.concatenate([x[:, :TILE].astype(BF16) for x in ra], axis=0)
            agg_ref[rows, :] = jnp.concatenate([x[:, TILE:].astype(BF16) for x in ra], axis=0)
            both = jnp.concatenate([s, r], axis=1)
            tab = jnp.concatenate([tab_ref[first + n] for n in range(4)], axis=1)
            fsr_acc[...] += mm(tab, both)
            return rows, both

        def own(at, _):
            rows, both = owned(at)
            own_ref[rows, :] = mmt(both, wsr)
            return 0

        lax.fori_loop(0, OWN_BLOCKS // 4, own, 0)
        _, both = owned(OWN_BLOCKS // 4)
        back = mmt(wsr, both).astype(BF16)
        for n in range(MIG_BLOCKS):
            far_ref[n] = back[:, n * TILE : (n + 1) * TILE]

        def halo(at, _):
            first = OWNED_BLOCKS + at * 4
            s = jnp.concatenate([s_acc[first + n].astype(BF16) for n in range(4)], axis=0)
            back = mmt(ws, s).astype(BF16)
            for n in range(4):
                far_ref[first - OWN_BLOCKS + n] = back[:, n * TILE : (n + 1) * TILE]
            tab = jnp.concatenate([tab_ref[first + n] for n in range(4)], axis=1)
            fsr_acc[:, :TILE] += mm(tab, s)
            return 0

        lax.fori_loop(0, HALO_BLOCKS // 4, halo, 0)
        first = fsr_acc[:, :TILE]
        second = fsr_acc[:, TILE:]
        edge_part = fe_acc[...].T
        w2_part = w2_acc[...]
        g_row = jnp.sum(g_acc[...].T, axis=0, keepdims=True)
        g_tile = jnp.broadcast_to(g_row, (CHUNK - WEIGHT_CHUNK, TILE))
        per = TILE // WEIGHT_CHUNK
        for n, part in enumerate((edge_part, first, second, w2_part)):
            for c in range(per):
                pay_ref[n * per + c, :WEIGHT_CHUNK, :] = part[
                    c * WEIGHT_CHUNK : (c + 1) * WEIGHT_CHUNK
                ]
                pay_ref[n * per + c, WEIGHT_CHUNK:, :] = g_tile


def edge_pass(meta, edges, cot_edge, send_idx, recv_idx, table, cot_agg, w_first, w_second, gain):
    rows = GROUPS * GROUP * TILE
    steps = edges.shape[0] // rows
    block = (TILE, TILE)

    def whole(*shape):
        return pl.BlockSpec(shape, lambda s, m: (0,) * len(shape))

    stream = pl.BlockSpec((rows, TILE), lambda s, m: (s, 0))
    return pl.pallas_call(
        edge_kernel,
        name="edge_block",
        grid_spec=pltpu.PrefetchScalarGridSpec(
            num_scalar_prefetch=1,
            grid=(steps,),
            in_specs=[
                stream,
                stream,
                whole(*send_idx.shape),
                whole(*recv_idx.shape),
                whole(*table.shape),
                whole(*cot_agg.shape),
                whole(*w_first.shape),
                whole(*w_second.shape),
                whole(*gain.shape),
            ],
            out_specs=[
                stream,
                stream,
                whole(OWNED_BLOCKS * TILE, TILE),
                whole(FAR_BLOCKS, TILE, TILE),
                whole(OWN_BLOCKS * TILE, TILE),
                whole(RANKS, CHUNK, TILE),
            ],
            scratch_shapes=[
                pltpu.VMEM((TABLE_BLOCKS,) + block, BF16),
                pltpu.VMEM((OWNED_BLOCKS,) + block, BF16),
                pltpu.VMEM((OWNED_BLOCKS,) + block, BF16),
                pltpu.VMEM((TABLE_BLOCKS,) + block, F32),
                pltpu.VMEM((OWNED_BLOCKS, TILE, 2 * TILE), F32),
                pltpu.VMEM(block, F32),
                pltpu.VMEM(block, F32),
                pltpu.VMEM(block, F32),
                pltpu.VMEM(block, F32),
                pltpu.VMEM((3,) + block, BF16),
                pltpu.VMEM(block, BF16),
                pltpu.VMEM((TILE, 2 * TILE), F32),
            ],
        ),
        out_shape=[
            jax.ShapeDtypeStruct(edges.shape, BF16),
            jax.ShapeDtypeStruct(edges.shape, BF16),
            jax.ShapeDtypeStruct((OWNED_BLOCKS * TILE, TILE), BF16),
            jax.ShapeDtypeStruct((FAR_BLOCKS, TILE, TILE), BF16),
            jax.ShapeDtypeStruct((OWN_BLOCKS * TILE, TILE), F32),
            jax.ShapeDtypeStruct((RANKS, CHUNK, TILE), F32),
        ],
        compiler_params=pltpu.CompilerParams(vmem_limit_bytes=VMEM_LIMIT),
        cost_estimate=pl.CostEstimate(
            flops=12 * 10**9, bytes_accessed=24 * 2**20, transcendentals=3 * 2**20
        ),
    )(meta, edges, cot_edge, send_idx, recv_idx, table, cot_agg, w_first, w_second, gain)


def rank_device(rank):
    i = lax.axis_index("gx")
    j = lax.axis_index("gy")
    gx = (rank // 8) * 4 + (lax.rem(i, 4) // 2) * 2 + lax.rem(rank, 2)
    gy = lax.rem(rank // 2, 4) * 2 + lax.rem(j, 2)
    return gx, gy


def my_rank():
    i = lax.axis_index("gx")
    j = lax.axis_index("gy")
    return (i // 4) * 8 + (j // 2) * 2 + lax.rem(i, 2)


def column_device(place):
    i = lax.axis_index("gx")
    j = lax.axis_index("gy")
    return (i // 4) * 4 + (place // 2) * 2 + lax.rem(i, 2), (j // 2) * 2 + lax.rem(place, 2)


def my_place():
    i = lax.axis_index("gx")
    j = lax.axis_index("gy")
    return (lax.rem(i, 4) // 2) * 2 + lax.rem(j, 2)


def return_kernel(
    far_ref, pay_ref, send_ref, count_ref, halo_ref,
    acc, sum_ref,
    back, mine, ring, col, got, pay_sem,
    send_sem, recv_sem, rs_send, rs_recv, col_send, col_recv, ag_send, ag_recv,
):
    rank = my_rank()
    place = my_place()
    barrier = pltpu.get_barrier_semaphore()
    greet_neighbours(barrier)

    def greet(s, _):
        device = rank_device(lax.rem(rank + s, RANKS))
        pl.semaphore_signal(barrier, inc=1, device_id=device, device_id_type=MESH)
        return 0

    lax.fori_loop(1, RANKS, greet, 0)
    for s in range(1, 4):
        device = column_device(lax.rem(place + s, 4))
        pl.semaphore_signal(barrier, inc=1, device_id=device, device_id_type=MESH)

    pay_copy = pltpu.make_async_copy(pay_ref.at[rank], ring.at[rank], pay_sem)
    pay_copy.start()
    acc[...] = jnp.zeros_like(acc)
    pl.semaphore_wait(barrier, neighbour_count() + RANKS - 1 + 3)

    def give(k, run, to_slot):
        return far_copy(far_ref, back, send_sem, recv_sem, k, run, 0, to_slot)

    def scatter_copy(s):
        to = lax.rem(rank + s, RANKS)
        return pltpu.make_async_remote_copy(
            src_ref=pay_ref.at[to],
            dst_ref=ring.at[rank],
            send_sem=rs_send.at[s],
            recv_sem=rs_recv.at[s],
            device_id=rank_device(to),
            device_id_type=MESH,
        )

    def start_scatter(s, _):
        scatter_copy(s).start()
        return 0

    lax.fori_loop(1, RANKS, start_scatter, 0)

    def start_give(order):
        for k, run in order:
            copy, exists = give(k, run, k ^ 1)
            guarded(exists, copy.start)

    start_give(ORDER[:X_END])

    def wait_scatter(s, _):
        scatter_copy(s).wait()
        return 0

    lax.fori_loop(1, RANKS, wait_scatter, 0)

    pay_copy.wait()

    def add_up(s, total):
        return total + ring[s]

    col[0] = lax.fori_loop(1, RANKS, add_up, ring[0], unroll=8)

    def column_copy(s):
        return pltpu.make_async_remote_copy(
            src_ref=col.at[0],
            dst_ref=col.at[s],
            send_sem=col_send.at[s],
            recv_sem=col_recv.at[s],
            device_id=column_device(lax.rem(place + s, 4)),
            device_id_type=MESH,
        )

    for s in range(1, 4):
        column_copy(s).start()
    start_give(ORDER[X_END:])

    slot = lax.broadcasted_iota(jnp.int32, (1, TILE), 1)

    def spread(index, values_t):
        upper = jnp.broadcast_to(index >= HALF, values_t.shape)
        none = jnp.zeros((), BF16)
        right = jnp.concatenate(
            [jnp.where(upper, none, values_t), jnp.where(upper, values_t, none)], axis=0
        )
        low = jnp.where(index >= HALF, index - HALF, index)
        right = right.T

        def piece(m, _):
            first = pl.multiple_of(m * 2 * TILE, 2 * TILE)
            hot = onehot(2 * TILE, low, first)
            acc[pl.ds(first, 2 * TILE), :] += mm(hot, right)
            return 0

        lax.fori_loop(0, HALF // (2 * TILE), piece, 0, unroll=8)

    for k in range(4):
        copy, exists = give(k, 0, k)
        guarded(exists, copy.wait_recv)
        copy, exists = give(k, 0, k ^ 1)
        guarded(exists, copy.wait_send)
    indices, values = [], []
    for k in range(4):
        _, exists = neighbour(k)
        live = slot < count_ref[k]
        if exists is not None:
            live = jnp.logical_and(live, exists)
        indices.append(jnp.where(live, send_ref[pl.ds(k, 1), :], -1))
        blockv = back[k]
        if exists is not None:
            blockv = jnp.where(jnp.broadcast_to(live, (TILE, TILE)), blockv, jnp.zeros((), BF16))
        values.append(blockv)
    spread(jnp.concatenate(indices, axis=1), jnp.concatenate(values, axis=1))

    def take_all(order):
        for k, run in order:
            at, count = RUNS[k][run]
            copy, exists = give(k, run, k)

            def take(copy=copy, k=k, at=at, count=count):
                copy.wait_recv()
                first = table_place(k, at)
                index = halo_ref[pl.ds(k, 1), pl.ds((at - 1) * TILE, count * TILE)]
                spread(index, jnp.concatenate([back[first + n] for n in range(count)], axis=1))

            guarded(exists, take)

    take_all(ORDER[4:X_END])
    for s in range(1, 4):
        column_copy(s).wait()
    total = (col[0] + col[2]) + (col[1] + col[3])
    mine[...] = total[:WEIGHT_CHUNK]
    got[rank] = total[:WEIGHT_CHUNK]
    sum_ref[pl.ds(RANKS * WEIGHT_CHUNK, CHUNK - WEIGHT_CHUNK), :] = total[WEIGHT_CHUNK:]

    def gather_copy(s, owner):
        return pltpu.make_async_remote_copy(
            src_ref=mine,
            dst_ref=got.at[owner],
            send_sem=ag_send.at[s],
            recv_sem=ag_recv.at[s],
            device_id=rank_device(lax.rem(rank + s, RANKS)),
            device_id_type=MESH,
        )

    def start_gather(s, _):
        gather_copy(s, rank).start()
        return 0

    lax.fori_loop(1, RANKS, start_gather, 0)

    take_all(ORDER[X_END:])
    for k, run in ORDER[4:]:
        copy, exists = give(k, run, k ^ 1)
        guarded(exists, copy.wait_send)

    def wait_gather(s, _):
        owner = lax.rem(rank + RANKS - s, RANKS)
        gather_copy(s, owner).wait()
        return 0

    lax.fori_loop(1, RANKS, wait_gather, 0)
    for c in range(RANKS):
        sum_ref[c * WEIGHT_CHUNK : (c + 1) * WEIGHT_CHUNK, :] = got[c]


def give_back(far, payload, send_rows, counts, halo_rows):
    vmem = pl.BlockSpec(memory_space=pltpu.VMEM)
    smem = pl.BlockSpec(memory_space=pltpu.SMEM)
    hbm = pl.BlockSpec(memory_space=pl.ANY)
    dma = pltpu.SemaphoreType.DMA
    return pl.pallas_call(
        return_kernel,
        name="return_rows",
        out_shape=(
            jax.ShapeDtypeStruct((HALF, 2 * TILE), F32),
            jax.ShapeDtypeStruct((RANKS * WEIGHT_CHUNK + CHUNK - WEIGHT_CHUNK, TILE), F32),
        ),
        in_specs=[hbm, hbm, vmem, smem, vmem],
        out_specs=(vmem, vmem),
        scratch_shapes=[
            pltpu.VMEM((FAR_BLOCKS, TILE, TILE), BF16),
            pltpu.VMEM((WEIGHT_CHUNK, TILE), F32),
            pltpu.VMEM((RANKS, CHUNK, TILE), F32),
            pltpu.VMEM((4, CHUNK, TILE), F32),
            pltpu.VMEM((RANKS, WEIGHT_CHUNK, TILE), F32),
            dma,
            dma((4, MOST_RUNS)),
            dma((4, MOST_RUNS)),
            dma((RANKS,)),
            dma((RANKS,)),
            dma((4,)),
            dma((4,)),
            dma((RANKS,)),
            dma((RANKS,)),
        ],
        compiler_params=pltpu.CompilerParams(
            collective_id=1, has_side_effects=True, vmem_limit_bytes=RETURN_LIMIT
        ),
        cost_estimate=pl.CostEstimate(
            flops=5 * 10**9, bytes_accessed=8 * 2**20, transcendentals=0
        ),
    )(far, payload, send_rows, counts, halo_rows)


def per_device(
    latent,
    edge_state,
    w_first,
    w_second,
    norm_gain,
    send_list,
    send_count,
    halo_list,
    senders,
    receivers,
    cotangent_edge,
    cotangent_agg,
):
    send_rows = send_list[0, 0]
    halo_rows = halo_list[0, 0]
    counts = send_count[0, 0]
    send_idx = senders.reshape(-1, TILE)
    recv_idx = receivers.reshape(-1, TILE)
    table, meta = fetch(latent[0, 0], send_rows, counts, halo_rows, send_idx, recv_idx)
    new_edge, grad_edge, aggregate, far, own, payload = edge_pass(
        meta,
        edge_state[0, 0],
        cotangent_edge[0, 0],
        send_idx,
        recv_idx,
        table,
        cotangent_agg[0, 0],
        w_first,
        w_second,
        norm_gain.reshape(1, TILE),
    )
    returned, sums = give_back(far, payload, send_rows, counts, halo_rows)
    grad_latent = own + jnp.concatenate([returned[:, :TILE], returned[:, TILE:]], axis=0)
    return (
        new_edge[None, None],
        aggregate[None, None],
        grad_edge[None, None],
        grad_latent[None, None],
        sums[: 3 * TILE],
        sums[3 * TILE : 4 * TILE],
        sums[4 * TILE],
    )


def solution(mesh):
    rows = P("gx", "gy", None, None)
    flat = P("gx", "gy", None)
    in_specs = (rows, rows, P(), P(), P(), rows, flat, rows, flat, flat, rows, rows)
    out_specs = (rows, rows, rows, rows, P(), P(), P())
    return jax.shard_map(
        per_device, mesh=mesh, in_specs=in_specs, out_specs=out_specs, check_vma=False
    )
```

```python
import functools

import jax
import jax.numpy as jnp
from jax import lax
from jax.experimental import pallas as pl
from jax.experimental.pallas import tpu as pltpu
from jax.sharding import PartitionSpec as P

MESH = pl.DeviceIdType.MESH
F32 = jnp.float32
BF16 = jnp.bfloat16
TILE = 128
EPS = 1e-05
N_GX = 16
N_GY = 8
OWN_BLOCKS = 32
MIG_BLOCKS = 4
HALO_BLOCKS = 32
OWNED_BLOCKS = OWN_BLOCKS + MIG_BLOCKS
FAR_BLOCKS = MIG_BLOCKS + HALO_BLOCKS
TABLE_BLOCKS = OWN_BLOCKS + FAR_BLOCKS
PER_DIR = HALO_BLOCKS // 4
HALF = OWN_BLOCKS * TILE // 2
GROUP = 16
GROUPS = 1
UNROLL = 1
RANKS = 32
CHUNK = 24
VMEM_LIMIT = 62 * 2**20
RETURN_LIMIT = 24 * 2**20
EDGE_LIMIT = 48 * 2**20
WEIGHT_CHUNK = 16


def mm(a, b):
    return jnp.dot(a, b, preferred_element_type=F32)


def mmt(a, b):
    return lax.dot_general(a, b, (((1,), (1,)), ((), ())), preferred_element_type=F32)


def onehot(rows, row_index, base):
    lanes = row_index.shape[1]
    row = lax.broadcasted_iota(jnp.int16, (rows, lanes), 0)
    index = jnp.broadcast_to((row_index - base).astype(jnp.int16), (rows, lanes))
    return jnp.where(row == index, jnp.ones((), BF16), jnp.zeros((), BF16))


def neighbour(k):
    i = lax.axis_index("gx")
    j = lax.axis_index("gy")
    if k == 0:
        return (lax.rem(i + N_GX - 1, N_GX), j), None
    if k == 1:
        return (lax.rem(i + 1, N_GX), j), None
    if k == 2:
        return (i, j - 1), j > 0
    return (i, j + 1), j < N_GY - 1


def guarded(exists, action):
    if exists is None:
        action()
    else:
        pl.when(exists)(action)


def greet_neighbours(barrier):
    for k in range(4):
        device, exists = neighbour(k)

        def signal(device=device):
            pl.semaphore_signal(barrier, inc=1, device_id=device, device_id_type=MESH)

        guarded(exists, signal)


def neighbour_count():
    j = lax.axis_index("gy")
    return 2 + jnp.where(j > 0, 1, 0) + jnp.where(j < N_GY - 1, 1, 0)


X_RUNS = ((0, 1), (1, 4), (5, 4))
Y_RUNS = ((0, 1), (1, 4), (5, 2), (7, 2))
RUNS = (X_RUNS, X_RUNS, Y_RUNS, Y_RUNS)
MOST_RUNS = 4
LONGEST = 4
ORDER = (
    [(k, 0) for k in (2, 3, 0, 1)]
    + [(k, run) for run in (1, 2) for k in (0, 1)]
    + [(k, run) for run in (1, 2, 3) for k in (2, 3)]
)
X_END = 4 + 4


def table_place(direction, at):
    if at == 0:
        return direction
    return MIG_BLOCKS + direction * PER_DIR + at - 1


def far_copy(src, dst, send_sem, recv_sem, k, run, base, to_slot):
    at, count = RUNS[k][run]
    device, exists = neighbour(k)
    copy = pltpu.make_async_remote_copy(
        src_ref=src.at[pl.ds(table_place(k, at), count)],
        dst_ref=dst.at[pl.ds(base + table_place(to_slot, at), count)],
        send_sem=send_sem.at[k, run],
        recv_sem=recv_sem.at[to_slot, run],
        device_id=device,
        device_id_type=MESH,
    )
    return copy, exists


def fetch_kernel(
    lat_ref, send_ref, count_ref, halo_ref, snd_ref, rcv_ref, w1_ref, cota_ref,
    tab_ref, ps_ref, pr_ref, ca_ref, meta_ref,
    lat_t, out_buf, far_in, ps_buf, pr_buf, ca_buf,
    send_sem, recv_sem, tab_sem, ps_sem, own_sem,
):
    barrier = pltpu.get_barrier_semaphore()
    greet_neighbours(barrier)

    def turn(b, _):
        rows = lat_ref[pl.ds(pl.multiple_of(b * TILE, TILE), TILE), :]
        lat_t[b] = rows.T
        return 0

    lax.fori_loop(0, OWN_BLOCKS, turn, 0, unroll=8)
    own_tab = pltpu.make_async_copy(lat_t, tab_ref.at[pl.ds(0, OWN_BLOCKS)], own_sem.at[0])
    own_tab.start()
    half = OWN_BLOCKS // 2

    def pick(index):
        low = jnp.where(index >= HALF, index - HALF, index)
        acc = None
        for piece in range(half // 2):
            hot = onehot(2 * TILE, low, piece * 2 * TILE)
            left = jnp.concatenate(
                [
                    jnp.concatenate([lat_t[2 * piece], lat_t[2 * piece + 1]], axis=1),
                    jnp.concatenate([lat_t[half + 2 * piece], lat_t[half + 2 * piece + 1]], axis=1),
                ],
                axis=0,
            )
            part = mm(left, hot)
            acc = part if acc is None else acc + part
        upper = jnp.broadcast_to(index >= HALF, (TILE, index.shape[1]))
        return jnp.where(upper, acc[TILE:], acc[:TILE]).astype(BF16)

    slot = lax.broadcasted_iota(jnp.int32, (1, TILE), 1)

    def live_index(k):
        return jnp.where(slot < count_ref[k], send_ref[pl.ds(k, 1), :], -1)

    for pair in range(2):
        index = jnp.concatenate([live_index(2 * pair), live_index(2 * pair + 1)], axis=1)
        rows = pick(index)
        out_buf[2 * pair] = rows[:, :TILE]
        out_buf[2 * pair + 1] = rows[:, TILE:]

    pl.semaphore_wait(barrier, neighbour_count())

    for k, run in ORDER:
        at, count = RUNS[k][run]
        if at:

            def gather(step, _, k=k, at=at):
                first = pl.multiple_of((at - 1) * TILE + step * 2 * TILE, 2 * TILE)
                rows = pick(halo_ref[pl.ds(k, 1), pl.ds(first, 2 * TILE)])
                place = table_place(k, at) + 2 * step
                out_buf[place] = rows[:, :TILE]
                out_buf[place + 1] = rows[:, TILE:]
                return 0

            lax.fori_loop(0, count // 2, gather, 0)
        copy, exists = far_copy(out_buf, far_in, send_sem, recv_sem, k, run, 0, k ^ 1)
        guarded(exists, copy.start)

    for k in (2, 3):
        _, exists = neighbour(k)

        def fill(k=k):
            for at, count in RUNS[k]:
                first = table_place(k, at)
                far_in[first : first + count] = jnp.zeros((count, TILE, TILE), BF16)

        pl.when(jnp.logical_not(exists))(fill)

    firsts = lax.shift_right_logical(
        jnp.concatenate([snd_ref[...].T[:1], rcv_ref[...].T[:1]], axis=0), 7
    )
    meta_ref[...] = firsts
    ws_t = w1_ref[TILE : 2 * TILE, :].T
    both_t = jnp.concatenate([ws_t, w1_ref[2 * TILE :, :].T], axis=0)

    def turn_cotangents(at, _):
        first = at * 4
        rows = pl.ds(pl.multiple_of(first * TILE, 4 * TILE), 4 * TILE)
        turned = cota_ref[rows, :].T
        for n in range(4):
            ca_buf[first + n] = turned[:, n * TILE : (n + 1) * TILE]
        return 0

    lax.fori_loop(0, OWNED_BLOCKS // 4, turn_cotangents, 0)
    own_ca = pltpu.make_async_copy(ca_buf, ca_ref, own_sem.at[1])
    own_ca.start()

    def project_both(source, first, place):
        blocks = jnp.concatenate([source[first + n] for n in range(4)], axis=1)
        out = mm(both_t, blocks).astype(BF16)
        for n in range(4):
            ps_buf[place + n] = out[:TILE, n * TILE : (n + 1) * TILE]
            pr_buf[place + n] = out[TILE:, n * TILE : (n + 1) * TILE]

    def project_own(at, _):
        project_both(lat_t, at * 4, at * 4)
        return 0

    lax.fori_loop(0, OWN_BLOCKS // 4, project_own, 0)
    own_ps = pltpu.make_async_copy(
        ps_buf.at[pl.ds(0, OWN_BLOCKS)], ps_ref.at[pl.ds(0, OWN_BLOCKS)], own_sem.at[2]
    )
    own_ps.start()

    def arrived(k, run):
        copy, exists = far_copy(out_buf, far_in, send_sem, recv_sem, k, run, 0, k)
        guarded(exists, copy.wait_recv)

    for k in range(4):
        arrived(k, 0)
    project_both(far_in, 0, OWN_BLOCKS)
    own_pr = pltpu.make_async_copy(pr_buf, pr_ref, own_sem.at[3])
    own_pr.start()
    mig_ps = pltpu.make_async_copy(
        ps_buf.at[pl.ds(OWN_BLOCKS, MIG_BLOCKS)], ps_ref.at[pl.ds(OWN_BLOCKS, MIG_BLOCKS)],
        own_sem.at[4],
    )
    mig_ps.start()
    mig_tab = pltpu.make_async_copy(
        far_in.at[pl.ds(0, MIG_BLOCKS)], tab_ref.at[pl.ds(OWN_BLOCKS, MIG_BLOCKS)], own_sem.at[5]
    )
    mig_tab.start()
    copies = [own_tab, own_ca, own_ps, own_pr, mig_ps, mig_tab]

    for k, run in ORDER[4:]:
        at, count = RUNS[k][run]
        arrived(k, run)
        first = table_place(k, at)
        place = OWN_BLOCKS + first
        tab_copy = pltpu.make_async_copy(
            far_in.at[pl.ds(first, count)], tab_ref.at[pl.ds(place, count)], tab_sem.at[k, run]
        )
        tab_copy.start()
        blocks = jnp.concatenate([far_in[first + n] for n in range(count)], axis=1)
        out = mm(ws_t, blocks).astype(BF16)
        for n in range(count):
            ps_buf[place + n] = out[:, n * TILE : (n + 1) * TILE]
        ps_copy = pltpu.make_async_copy(
            ps_buf.at[pl.ds(place, count)], ps_ref.at[pl.ds(place, count)], ps_sem.at[k, run]
        )
        ps_copy.start()
        copies += [tab_copy, ps_copy]

    for k, run in ORDER:
        copy, exists = far_copy(out_buf, far_in, send_sem, recv_sem, k, run, 0, k ^ 1)
        guarded(exists, copy.wait_send)
    for copy in copies:
        copy.wait()


def fetch(nodes, send_rows, counts, halo_rows, send_idx, recv_idx, w_first, cot_agg):
    vmem = pl.BlockSpec(memory_space=pltpu.VMEM)
    smem = pl.BlockSpec(memory_space=pltpu.SMEM)
    hbm = pl.BlockSpec(memory_space=pl.ANY)
    dma = pltpu.SemaphoreType.DMA
    block = (TILE, TILE)
    return pl.pallas_call(
        fetch_kernel,
        name="fetch_rows",
        out_shape=(
            jax.ShapeDtypeStruct((TABLE_BLOCKS,) + block, BF16),
            jax.ShapeDtypeStruct((TABLE_BLOCKS,) + block, BF16),
            jax.ShapeDtypeStruct((OWNED_BLOCKS,) + block, BF16),
            jax.ShapeDtypeStruct((OWNED_BLOCKS,) + block, BF16),
            jax.ShapeDtypeStruct((2, TILE), jnp.int32),
        ),
        in_specs=[vmem, vmem, smem, vmem, vmem, vmem, vmem, vmem],
        out_specs=(hbm, hbm, hbm, hbm, vmem),
        scratch_shapes=[
            pltpu.VMEM((OWN_BLOCKS,) + block, BF16),
            pltpu.VMEM((FAR_BLOCKS,) + block, BF16),
            pltpu.VMEM((FAR_BLOCKS,) + block, BF16),
            pltpu.VMEM((TABLE_BLOCKS,) + block, BF16),
            pltpu.VMEM((OWNED_BLOCKS,) + block, BF16),
            pltpu.VMEM((OWNED_BLOCKS,) + block, BF16),
            dma((4, MOST_RUNS)),
            dma((4, MOST_RUNS)),
            dma((4, MOST_RUNS)),
            dma((4, MOST_RUNS)),
            dma((6,)),
        ],
        compiler_params=pltpu.CompilerParams(
            collective_id=0, has_side_effects=True, vmem_limit_bytes=VMEM_LIMIT
        ),
        cost_estimate=pl.CostEstimate(
            flops=5 * 10**9, bytes_accessed=8 * 2**20, transcendentals=0
        ),
    )(nodes, send_rows, counts, halo_rows, send_idx, recv_idx, w_first, cot_agg)


def edge_kernel(
    meta_ref, edge_ref, cot_ref, snd_ref, rcv_ref, tab_hbm, ps_t, pr_t, ca_t,
    w1_ref, w2_ref, gain_ref,
    new_ref, grad_ref, agg_ref, far_ref, own_ref, pay_ref,
    tab_ref, s_acc, ra_acc, fe_acc, w2_acc, g_acc, gain_b, w1_t, w2_t, fsr_acc, tab_sem,
):
    step = pl.program_id(0)
    steps = pl.num_programs(0)

    tab_copy = pltpu.make_async_copy(tab_hbm, tab_ref, tab_sem)

    @pl.when(step == 0)
    def _prologue():
        tab_copy.start()
        w1_t[...] = w1_ref[:TILE, :].T
        w2_t[...] = w2_ref[...].T
        gain_b[...] = jnp.broadcast_to(gain_ref[...], (TILE, TILE)).T

        def zero(b, _):
            s_acc[b] = jnp.zeros((TILE, TILE), F32)
            return 0

        lax.fori_loop(0, TABLE_BLOCKS, zero, 0, unroll=2)

        def zero_two(b, _):
            ra_acc[b] = jnp.zeros((TILE, 2 * TILE), F32)
            return 0

        lax.fori_loop(0, OWNED_BLOCKS, zero_two, 0, unroll=2)
        fe_acc[...] = jnp.zeros_like(fe_acc)
        w2_acc[...] = jnp.zeros_like(w2_acc)
        g_acc[...] = jnp.zeros_like(g_acc)

    we = w1_ref[:TILE, :]
    we_t = w1_t[...]
    w2 = w2_ref[...]
    gain = jnp.concatenate([gain_b[...]] * GROUP, axis=1)
    wide = GROUP * TILE

    def group(p, _):
        tile = (step * GROUPS + p) * GROUP
        first = pl.multiple_of(p * wide, wide)
        rows = pl.ds(first, wide)
        edges = edge_ref[rows, :]
        cot_t = cot_ref[rows, :].T.astype(F32)
        hot_s, hot_r, near, cots, blocks = [], [], [], [], []
        for side in range(GROUP):
            bs = meta_ref[0, tile + side]
            br = meta_ref[1, tile + side]
            blocks.append((bs, br))
            hs = onehot(TILE, snd_ref[pl.ds(tile + side, 1), :] & (TILE - 1), 0)
            hr = onehot(TILE, rcv_ref[pl.ds(tile + side, 1), :] & (TILE - 1), 0)
            hot_s.append(hs)
            hot_r.append(hr)
            near.append(
                mm(
                    jnp.concatenate([ps_t[bs], pr_t[br]], axis=1),
                    jnp.concatenate([hs, hr], axis=0),
                )
            )
            cots.append(mm(ca_t[br], hr))
        preact = mmt(we_t, edges) + jnp.concatenate(near, axis=1)
        sig = 0.5 * jnp.tanh(0.5 * preact) + 0.5
        hidden = preact * sig
        slope = sig + hidden * (1.0 - sig)
        hidden = hidden.astype(BF16)
        output = mm(w2_t[...], hidden)
        centred = output - jnp.sum(output, axis=0, keepdims=True) * (1.0 / TILE)
        variance = jnp.sum(centred * centred, axis=0, keepdims=True) * (1.0 / TILE)
        inverse = lax.rsqrt(variance + EPS)
        normed = centred * inverse
        message = normed * gain
        message = message.astype(BF16)
        new_ref[rows, :] = (edges.astype(F32) + message.T.astype(F32)).astype(BF16)
        d_message = cot_t + jnp.concatenate(cots, axis=1)
        weighted = d_message * normed
        g_sum = weighted[:, :TILE]
        for side in range(1, GROUP):
            g_sum += weighted[:, side * TILE : (side + 1) * TILE]
        g_acc[...] += g_sum
        d_norm = d_message * gain
        mean_one = jnp.sum(d_norm, axis=0, keepdims=True) * (1.0 / TILE)
        mean_two = jnp.sum(weighted * gain, axis=0, keepdims=True) * (1.0 / TILE)
        d_output = (inverse * (d_norm - mean_one - normed * mean_two)).astype(BF16)
        w2_acc[...] += mmt(hidden, d_output)
        d_preact = (mm(w2, d_output) * slope).astype(BF16)
        fe_acc[...] += mm(d_preact, edges)
        d_edge = mm(we, d_preact).astype(BF16)
        grad_ref[rows, :] = (cot_ref[rows, :].astype(F32) + d_edge.T.astype(F32)).astype(BF16)
        for side in range(GROUP):
            bs, br = blocks[side]
            lanes = slice(side * TILE, (side + 1) * TILE)
            d_pre = d_preact[:, lanes]
            s_acc[bs] += mmt(hot_s[side], d_pre)
            both = jnp.concatenate([d_pre, message[:, lanes]], axis=0)
            ra_acc[br] += mmt(hot_r[side], both)
        return 0

    lax.fori_loop(0, GROUPS, group, 0, unroll=UNROLL)

    @pl.when(step == steps - 1)
    def _epilogue():
        tab_copy.wait()
        ws = w1_ref[TILE : 2 * TILE, :]
        wr = w1_ref[2 * TILE :, :]
        wsr = jnp.concatenate([ws, wr], axis=1)

        fsr_acc[...] = jnp.zeros_like(fsr_acc)

        def owned(at):
            first = at * 4
            rows = pl.ds(pl.multiple_of(first * TILE, 4 * TILE), 4 * TILE)
            s = jnp.concatenate([s_acc[first + n].astype(BF16) for n in range(4)], axis=0)
            ra = [ra_acc[first + n] for n in range(4)]
            r = jnp.concatenate([x[:, :TILE].astype(BF16) for x in ra], axis=0)
            agg_ref[rows, :] = jnp.concatenate([x[:, TILE:].astype(BF16) for x in ra], axis=0)
            both = jnp.concatenate([s, r], axis=1)
            tab = jnp.concatenate([tab_ref[first + n] for n in range(4)], axis=1)
            fsr_acc[...] += mm(tab, both)
            return rows, both

        def own(at, _):
            rows, both = owned(at)
            own_ref[rows, :] = both
            return 0

        lax.fori_loop(0, OWN_BLOCKS // 4, own, 0)
        _, both = owned(OWN_BLOCKS // 4)
        back = mmt(wsr, both).astype(BF16)
        for n in range(MIG_BLOCKS):
            far_ref[n] = back[:, n * TILE : (n + 1) * TILE]

        def halo(at, _):
            first = OWNED_BLOCKS + at * 4
            s = jnp.concatenate([s_acc[first + n].astype(BF16) for n in range(4)], axis=0)
            back = mmt(ws, s).astype(BF16)
            for n in range(4):
                far_ref[first - OWN_BLOCKS + n] = back[:, n * TILE : (n + 1) * TILE]
            tab = jnp.concatenate([tab_ref[first + n] for n in range(4)], axis=1)
            fsr_acc[:, :TILE] += mm(tab, s)
            return 0

        lax.fori_loop(0, HALO_BLOCKS // 4, halo, 0)
        first = fsr_acc[:, :TILE]
        second = fsr_acc[:, TILE:]
        edge_part = fe_acc[...].T
        w2_part = w2_acc[...]
        g_row = jnp.sum(g_acc[...].T, axis=0, keepdims=True)
        g_tile = jnp.broadcast_to(g_row, (CHUNK - WEIGHT_CHUNK, TILE))
        per = TILE // WEIGHT_CHUNK
        for n, part in enumerate((edge_part, first, second, w2_part)):
            for c in range(per):
                pay_ref[n * per + c, :WEIGHT_CHUNK, :] = part[
                    c * WEIGHT_CHUNK : (c + 1) * WEIGHT_CHUNK
                ]
                pay_ref[n * per + c, WEIGHT_CHUNK:, :] = g_tile


def edge_pass(
    meta, edges, cot_edge, send_idx, recv_idx, table, ps, pr, ca, w_first, w_second, gain
):
    rows = GROUPS * GROUP * TILE
    steps = edges.shape[0] // rows
    block = (TILE, TILE)

    def whole(*shape):
        return pl.BlockSpec(shape, lambda s, m: (0,) * len(shape))

    stream = pl.BlockSpec((rows, TILE), lambda s, m: (s, 0))
    return pl.pallas_call(
        edge_kernel,
        name="edge_block",
        grid_spec=pltpu.PrefetchScalarGridSpec(
            num_scalar_prefetch=1,
            grid=(steps,),
            in_specs=[
                stream,
                stream,
                whole(*send_idx.shape),
                whole(*recv_idx.shape),
                pl.BlockSpec(memory_space=pl.ANY),
                whole(*ps.shape),
                whole(*pr.shape),
                whole(*ca.shape),
                whole(*w_first.shape),
                whole(*w_second.shape),
                whole(*gain.shape),
            ],
            out_specs=[
                stream,
                stream,
                whole(OWNED_BLOCKS * TILE, TILE),
                whole(FAR_BLOCKS, TILE, TILE),
                whole(OWN_BLOCKS * TILE, 2 * TILE),
                whole(RANKS, CHUNK, TILE),
            ],
            scratch_shapes=[
                pltpu.VMEM((TABLE_BLOCKS,) + block, BF16),
                pltpu.VMEM((TABLE_BLOCKS,) + block, F32),
                pltpu.VMEM((OWNED_BLOCKS, TILE, 2 * TILE), F32),
                pltpu.VMEM(block, F32),
                pltpu.VMEM(block, F32),
                pltpu.VMEM(block, F32),
                pltpu.VMEM(block, F32),
                pltpu.VMEM(block, BF16),
                pltpu.VMEM(block, BF16),
                pltpu.VMEM((TILE, 2 * TILE), F32),
                pltpu.SemaphoreType.DMA,
            ],
        ),
        out_shape=[
            jax.ShapeDtypeStruct(edges.shape, BF16),
            jax.ShapeDtypeStruct(edges.shape, BF16),
            jax.ShapeDtypeStruct((OWNED_BLOCKS * TILE, TILE), BF16),
            jax.ShapeDtypeStruct((FAR_BLOCKS, TILE, TILE), BF16),
            jax.ShapeDtypeStruct((OWN_BLOCKS * TILE, 2 * TILE), BF16),
            jax.ShapeDtypeStruct((RANKS, CHUNK, TILE), F32),
        ],
        compiler_params=pltpu.CompilerParams(vmem_limit_bytes=EDGE_LIMIT),
        cost_estimate=pl.CostEstimate(
            flops=12 * 10**9, bytes_accessed=24 * 2**20, transcendentals=3 * 2**20
        ),
    )(meta, edges, cot_edge, send_idx, recv_idx, table, ps, pr, ca, w_first, w_second, gain)


def rank_device(rank):
    i = lax.axis_index("gx")
    j = lax.axis_index("gy")
    gx = (rank // 8) * 4 + (lax.rem(i, 4) // 2) * 2 + lax.rem(rank, 2)
    gy = lax.rem(rank // 2, 4) * 2 + lax.rem(j, 2)
    return gx, gy


def my_rank():
    i = lax.axis_index("gx")
    j = lax.axis_index("gy")
    return (i // 4) * 8 + (j // 2) * 2 + lax.rem(i, 2)


def column_device(place):
    i = lax.axis_index("gx")
    j = lax.axis_index("gy")
    return (i // 4) * 4 + (place // 2) * 2 + lax.rem(i, 2), (j // 2) * 2 + lax.rem(place, 2)


def my_place():
    i = lax.axis_index("gx")
    j = lax.axis_index("gy")
    return (lax.rem(i, 4) // 2) * 2 + lax.rem(j, 2)


def return_kernel(
    far_ref, own_ref, pay_ref, send_ref, count_ref, halo_ref, w1_ref,
    lat_ref, sum_ref,
    back, own_buf, mine, ring, col, got, pay_sem, own_sem,
    send_sem, recv_sem, rs_send, rs_recv, col_send, col_recv, ag_send, ag_recv,
):
    rank = my_rank()
    place = my_place()
    barrier = pltpu.get_barrier_semaphore()
    greet_neighbours(barrier)

    def greet(s, _):
        device = rank_device(lax.rem(rank + s, RANKS))
        pl.semaphore_signal(barrier, inc=1, device_id=device, device_id_type=MESH)
        return 0

    lax.fori_loop(1, RANKS, greet, 0)
    for s in range(1, 4):
        device = column_device(lax.rem(place + s, 4))
        pl.semaphore_signal(barrier, inc=1, device_id=device, device_id_type=MESH)

    pay_copy = pltpu.make_async_copy(pay_ref.at[rank], ring.at[rank], pay_sem)
    pay_copy.start()
    own_copy = pltpu.make_async_copy(own_ref, own_buf, own_sem)
    own_copy.start()
    pl.semaphore_wait(barrier, neighbour_count() + RANKS - 1 + 3)

    def give(k, run, to_slot):
        return far_copy(far_ref, back, send_sem, recv_sem, k, run, 0, to_slot)

    def scatter_copy(s):
        to = lax.rem(rank + s, RANKS)
        return pltpu.make_async_remote_copy(
            src_ref=pay_ref.at[to],
            dst_ref=ring.at[rank],
            send_sem=rs_send.at[s],
            recv_sem=rs_recv.at[s],
            device_id=rank_device(to),
            device_id_type=MESH,
        )

    def start_scatter(s, _):
        scatter_copy(s).start()
        return 0

    lax.fori_loop(1, RANKS, start_scatter, 0)

    def start_give(order):
        for k, run in order:
            copy, exists = give(k, run, k ^ 1)
            guarded(exists, copy.start)

    start_give(ORDER[:X_END])

    def wait_scatter(s, _):
        scatter_copy(s).wait()
        return 0

    own_copy.wait()
    wsr = jnp.concatenate([w1_ref[TILE : 2 * TILE, :], w1_ref[2 * TILE :, :]], axis=1)

    def own_part(m, _):
        rows = pl.ds(pl.multiple_of(m * 4 * TILE, 4 * TILE), 4 * TILE)
        lat_ref[rows, :] = mmt(own_buf[rows, :], wsr)
        return 0

    lax.fori_loop(0, OWN_BLOCKS // 4, own_part, 0, unroll=2)
    lax.fori_loop(1, RANKS, wait_scatter, 0)

    pay_copy.wait()

    def add_up(s, total):
        return total + ring[s]

    col[0] = lax.fori_loop(1, RANKS, add_up, ring[0], unroll=8)

    def column_copy(s):
        return pltpu.make_async_remote_copy(
            src_ref=col.at[0],
            dst_ref=col.at[s],
            send_sem=col_send.at[s],
            recv_sem=col_recv.at[s],
            device_id=column_device(lax.rem(place + s, 4)),
            device_id_type=MESH,
        )

    for s in range(1, 4):
        column_copy(s).start()
    start_give(ORDER[X_END:])

    slot = lax.broadcasted_iota(jnp.int32, (1, TILE), 1)

    def spread(index, values_t):
        upper = jnp.broadcast_to(index >= HALF, values_t.shape)
        none = jnp.zeros((), BF16)
        right = jnp.concatenate(
            [jnp.where(upper, none, values_t), jnp.where(upper, values_t, none)], axis=0
        )
        low = jnp.where(index >= HALF, index - HALF, index)
        right = right.T

        def piece(m, _):
            first = pl.multiple_of(m * 2 * TILE, 2 * TILE)
            hot = onehot(2 * TILE, low, first)
            part = mm(hot, right)
            lat_ref[pl.ds(first, 2 * TILE), :] += part[:, :TILE]
            lat_ref[pl.ds(HALF + first, 2 * TILE), :] += part[:, TILE:]
            return 0

        lax.fori_loop(0, HALF // (2 * TILE), piece, 0, unroll=8)

    for k in range(4):
        copy, exists = give(k, 0, k)
        guarded(exists, copy.wait_recv)
        copy, exists = give(k, 0, k ^ 1)
        guarded(exists, copy.wait_send)
    indices, values = [], []
    for k in range(4):
        _, exists = neighbour(k)
        live = slot < count_ref[k]
        if exists is not None:
            live = jnp.logical_and(live, exists)
        indices.append(jnp.where(live, send_ref[pl.ds(k, 1), :], -1))
        blockv = back[k]
        if exists is not None:
            blockv = jnp.where(jnp.broadcast_to(live, (TILE, TILE)), blockv, jnp.zeros((), BF16))
        values.append(blockv)
    spread(jnp.concatenate(indices, axis=1), jnp.concatenate(values, axis=1))

    def take_all(order):
        for k, run in order:
            at, count = RUNS[k][run]
            copy, exists = give(k, run, k)

            def take(copy=copy, k=k, at=at, count=count):
                copy.wait_recv()
                first = table_place(k, at)
                index = halo_ref[pl.ds(k, 1), pl.ds((at - 1) * TILE, count * TILE)]
                spread(index, jnp.concatenate([back[first + n] for n in range(count)], axis=1))

            guarded(exists, take)

    take_all(ORDER[4:X_END])
    for s in range(1, 4):
        column_copy(s).wait()
    total = (col[0] + col[2]) + (col[1] + col[3])
    mine[...] = total[:WEIGHT_CHUNK]
    got[rank] = total[:WEIGHT_CHUNK]
    sum_ref[pl.ds(RANKS * WEIGHT_CHUNK, CHUNK - WEIGHT_CHUNK), :] = total[WEIGHT_CHUNK:]

    def gather_copy(s, owner):
        return pltpu.make_async_remote_copy(
            src_ref=mine,
            dst_ref=got.at[owner],
            send_sem=ag_send.at[s],
            recv_sem=ag_recv.at[s],
            device_id=rank_device(lax.rem(rank + s, RANKS)),
            device_id_type=MESH,
        )

    def start_gather(s, _):
        gather_copy(s, rank).start()
        return 0

    lax.fori_loop(1, RANKS, start_gather, 0)

    take_all(ORDER[X_END:])
    for k, run in ORDER[4:]:
        copy, exists = give(k, run, k ^ 1)
        guarded(exists, copy.wait_send)

    def wait_gather(s, _):
        owner = lax.rem(rank + RANKS - s, RANKS)
        gather_copy(s, owner).wait()
        return 0

    lax.fori_loop(1, RANKS, wait_gather, 0)
    for c in range(RANKS):
        sum_ref[c * WEIGHT_CHUNK : (c + 1) * WEIGHT_CHUNK, :] = got[c]


def give_back(far, own, payload, send_rows, counts, halo_rows, w_first):
    vmem = pl.BlockSpec(memory_space=pltpu.VMEM)
    smem = pl.BlockSpec(memory_space=pltpu.SMEM)
    hbm = pl.BlockSpec(memory_space=pl.ANY)
    dma = pltpu.SemaphoreType.DMA
    return pl.pallas_call(
        return_kernel,
        name="return_rows",
        out_shape=(
            jax.ShapeDtypeStruct((OWN_BLOCKS * TILE, TILE), F32),
            jax.ShapeDtypeStruct((RANKS * WEIGHT_CHUNK + CHUNK - WEIGHT_CHUNK, TILE), F32),
        ),
        in_specs=[hbm, hbm, hbm, vmem, smem, vmem, vmem],
        out_specs=(vmem, vmem),
        scratch_shapes=[
            pltpu.VMEM((FAR_BLOCKS, TILE, TILE), BF16),
            pltpu.VMEM((OWN_BLOCKS * TILE, 2 * TILE), BF16),
            pltpu.VMEM((WEIGHT_CHUNK, TILE), F32),
            pltpu.VMEM((RANKS, CHUNK, TILE), F32),
            pltpu.VMEM((4, CHUNK, TILE), F32),
            pltpu.VMEM((RANKS, WEIGHT_CHUNK, TILE), F32),
            dma,
            dma,
            dma((4, MOST_RUNS)),
            dma((4, MOST_RUNS)),
            dma((RANKS,)),
            dma((RANKS,)),
            dma((4,)),
            dma((4,)),
            dma((RANKS,)),
            dma((RANKS,)),
        ],
        compiler_params=pltpu.CompilerParams(
            collective_id=1, has_side_effects=True, vmem_limit_bytes=RETURN_LIMIT
        ),
        cost_estimate=pl.CostEstimate(
            flops=5 * 10**9, bytes_accessed=8 * 2**20, transcendentals=0
        ),
    )(far, own, payload, send_rows, counts, halo_rows, w_first)


def per_device(
    latent,
    edge_state,
    w_first,
    w_second,
    norm_gain,
    send_list,
    send_count,
    halo_list,
    senders,
    receivers,
    cotangent_edge,
    cotangent_agg,
):
    send_rows = send_list[0, 0]
    halo_rows = halo_list[0, 0]
    counts = send_count[0, 0]
    send_idx = senders.reshape(-1, TILE)
    recv_idx = receivers.reshape(-1, TILE)
    table, ps, pr, ca, meta = fetch(
        latent[0, 0], send_rows, counts, halo_rows, send_idx, recv_idx, w_first, cotangent_agg[0, 0]
    )
    new_edge, grad_edge, aggregate, far, own, payload = edge_pass(
        meta,
        edge_state[0, 0],
        cotangent_edge[0, 0],
        send_idx,
        recv_idx,
        table,
        ps,
        pr,
        ca,
        w_first,
        w_second,
        norm_gain.reshape(1, TILE),
    )
    grad_latent, sums = give_back(far, own, payload, send_rows, counts, halo_rows, w_first)
    return (
        new_edge[None, None],
        aggregate[None, None],
        grad_edge[None, None],
        grad_latent[None, None],
        sums[: 3 * TILE],
        sums[3 * TILE : 4 * TILE],
        sums[4 * TILE],
    )


def solution(mesh):
    rows = P("gx", "gy", None, None)
    flat = P("gx", "gy", None)
    in_specs = (rows, rows, P(), P(), P(), rows, flat, rows, flat, flat, rows, rows)
    out_specs = (rows, rows, rows, rows, P(), P(), P())
    return jax.shard_map(
        per_device, mesh=mesh, in_specs=in_specs, out_specs=out_specs, check_vma=False
    )
```

```python
import functools

import jax
import jax.numpy as jnp
from jax import lax
from jax.experimental import pallas as pl
from jax.experimental.pallas import tpu as pltpu
from jax.sharding import PartitionSpec as P

MESH = pl.DeviceIdType.MESH
F32 = jnp.float32
BF16 = jnp.bfloat16
TILE = 128
EPS = 1e-05
N_GX = 16
N_GY = 8
OWN_BLOCKS = 32
MIG_BLOCKS = 4
HALO_BLOCKS = 32
OWNED_BLOCKS = OWN_BLOCKS + MIG_BLOCKS
FAR_BLOCKS = MIG_BLOCKS + HALO_BLOCKS
TABLE_BLOCKS = OWN_BLOCKS + FAR_BLOCKS
PER_DIR = HALO_BLOCKS // 4
HALF = OWN_BLOCKS * TILE // 2
GROUP = 16
GROUPS = 1
UNROLL = 1
RANKS = 32
CHUNK = 24
VMEM_LIMIT = 62 * 2**20
RETURN_LIMIT = 24 * 2**20
EDGE_LIMIT = 48 * 2**20
WEIGHT_CHUNK = 16


def mm(a, b):
    return jnp.dot(a, b, preferred_element_type=F32)


def mmt(a, b):
    return lax.dot_general(a, b, (((1,), (1,)), ((), ())), preferred_element_type=F32)


def onehot(rows, row_index, base):
    lanes = row_index.shape[1]
    row = lax.broadcasted_iota(jnp.int16, (rows, lanes), 0)
    index = jnp.broadcast_to((row_index - base).astype(jnp.int16), (rows, lanes))
    return jnp.where(row == index, jnp.ones((), BF16), jnp.zeros((), BF16))


def neighbour(k):
    i = lax.axis_index("gx")
    j = lax.axis_index("gy")
    if k == 0:
        return (lax.rem(i + N_GX - 1, N_GX), j), None
    if k == 1:
        return (lax.rem(i + 1, N_GX), j), None
    if k == 2:
        return (i, j - 1), j > 0
    return (i, j + 1), j < N_GY - 1


def guarded(exists, action):
    if exists is None:
        action()
    else:
        pl.when(exists)(action)


def greet_neighbours(barrier):
    for k in range(4):
        device, exists = neighbour(k)

        def signal(device=device):
            pl.semaphore_signal(barrier, inc=1, device_id=device, device_id_type=MESH)

        guarded(exists, signal)


def neighbour_count():
    j = lax.axis_index("gy")
    return 2 + jnp.where(j > 0, 1, 0) + jnp.where(j < N_GY - 1, 1, 0)


X_RUNS = ((0, 1), (1, 4), (5, 4))
Y_RUNS = ((0, 1), (1, 4), (5, 2), (7, 2))
RUNS = (X_RUNS, X_RUNS, Y_RUNS, Y_RUNS)
MOST_RUNS = 4
LONGEST = 4
ORDER = (
    [(k, 0) for k in (2, 3, 0, 1)]
    + [(k, run) for run in (1, 2) for k in (0, 1)]
    + [(k, run) for run in (1, 2, 3) for k in (2, 3)]
)
X_END = 4 + 4


def table_place(direction, at):
    if at == 0:
        return direction
    return MIG_BLOCKS + direction * PER_DIR + at - 1


def far_copy(src, dst, send_sem, recv_sem, k, run, base, to_slot):
    at, count = RUNS[k][run]
    device, exists = neighbour(k)
    copy = pltpu.make_async_remote_copy(
        src_ref=src.at[pl.ds(table_place(k, at), count)],
        dst_ref=dst.at[pl.ds(base + table_place(to_slot, at), count)],
        send_sem=send_sem.at[k, run],
        recv_sem=recv_sem.at[to_slot, run],
        device_id=device,
        device_id_type=MESH,
    )
    return copy, exists


def fetch_kernel(
    lat_ref, send_ref, count_ref, halo_ref, snd_ref, rcv_ref, w1_ref, cota_ref,
    tab_ref, ps_ref, pr_ref, ca_ref, meta_ref,
    lat_t, out_buf, far_in, ps_buf, pr_buf, ca_buf,
    send_sem, recv_sem, tab_sem, ps_sem, own_sem,
):
    barrier = pltpu.get_barrier_semaphore()
    greet_neighbours(barrier)

    def turn(b, _):
        rows = lat_ref[pl.ds(pl.multiple_of(b * TILE, TILE), TILE), :]
        lat_t[b] = rows.T
        return 0

    lax.fori_loop(0, OWN_BLOCKS, turn, 0, unroll=8)
    own_tab = pltpu.make_async_copy(lat_t, tab_ref.at[pl.ds(0, OWN_BLOCKS)], own_sem.at[0])
    own_tab.start()
    half = OWN_BLOCKS // 2

    def pick(index):
        low = jnp.where(index >= HALF, index - HALF, index)
        acc = None
        for piece in range(half // 2):
            hot = onehot(2 * TILE, low, piece * 2 * TILE)
            left = jnp.concatenate(
                [
                    jnp.concatenate([lat_t[2 * piece], lat_t[2 * piece + 1]], axis=1),
                    jnp.concatenate([lat_t[half + 2 * piece], lat_t[half + 2 * piece + 1]], axis=1),
                ],
                axis=0,
            )
            part = mm(left, hot)
            acc = part if acc is None else acc + part
        upper = jnp.broadcast_to(index >= HALF, (TILE, index.shape[1]))
        return jnp.where(upper, acc[TILE:], acc[:TILE]).astype(BF16)

    slot = lax.broadcasted_iota(jnp.int32, (1, TILE), 1)

    def live_index(k):
        return jnp.where(slot < count_ref[k], send_ref[pl.ds(k, 1), :], -1)

    for pair in range(2):
        index = jnp.concatenate([live_index(2 * pair), live_index(2 * pair + 1)], axis=1)
        rows = pick(index)
        out_buf[2 * pair] = rows[:, :TILE]
        out_buf[2 * pair + 1] = rows[:, TILE:]

    pl.semaphore_wait(barrier, neighbour_count())

    for k, run in ORDER:
        at, count = RUNS[k][run]
        if at:

            def gather(step, _, k=k, at=at):
                first = pl.multiple_of((at - 1) * TILE + step * 2 * TILE, 2 * TILE)
                rows = pick(halo_ref[pl.ds(k, 1), pl.ds(first, 2 * TILE)])
                place = table_place(k, at) + 2 * step
                out_buf[place] = rows[:, :TILE]
                out_buf[place + 1] = rows[:, TILE:]
                return 0

            lax.fori_loop(0, count // 2, gather, 0)
        copy, exists = far_copy(out_buf, far_in, send_sem, recv_sem, k, run, 0, k ^ 1)
        guarded(exists, copy.start)

    for k in (2, 3):
        _, exists = neighbour(k)

        def fill(k=k):
            for at, count in RUNS[k]:
                first = table_place(k, at)
                far_in[first : first + count] = jnp.zeros((count, TILE, TILE), BF16)

        pl.when(jnp.logical_not(exists))(fill)

    firsts = lax.shift_right_logical(
        jnp.concatenate([snd_ref[...].T[:1], rcv_ref[...].T[:1]], axis=0), 7
    )
    meta_ref[...] = firsts
    ws_t = w1_ref[TILE : 2 * TILE, :].T
    both_t = jnp.concatenate([ws_t, w1_ref[2 * TILE :, :].T], axis=0)

    def turn_cotangents(at, _):
        first = at * 4
        rows = pl.ds(pl.multiple_of(first * TILE, 4 * TILE), 4 * TILE)
        turned = cota_ref[rows, :].T
        for n in range(4):
            ca_buf[first + n] = turned[:, n * TILE : (n + 1) * TILE]
        return 0

    lax.fori_loop(0, OWNED_BLOCKS // 4, turn_cotangents, 0)
    own_ca = pltpu.make_async_copy(ca_buf, ca_ref, own_sem.at[1])
    own_ca.start()

    def project_both(source, first, place):
        blocks = jnp.concatenate([source[first + n] for n in range(4)], axis=1)
        out = mm(both_t, blocks).astype(BF16)
        for n in range(4):
            ps_buf[place + n] = out[:TILE, n * TILE : (n + 1) * TILE]
            pr_buf[place + n] = out[TILE:, n * TILE : (n + 1) * TILE]

    def project_own(at, _):
        project_both(lat_t, at * 4, at * 4)
        return 0

    lax.fori_loop(0, OWN_BLOCKS // 4, project_own, 0)
    own_ps = pltpu.make_async_copy(
        ps_buf.at[pl.ds(0, OWN_BLOCKS)], ps_ref.at[pl.ds(0, OWN_BLOCKS)], own_sem.at[2]
    )
    own_ps.start()

    def arrived(k, run):
        copy, exists = far_copy(out_buf, far_in, send_sem, recv_sem, k, run, 0, k)
        guarded(exists, copy.wait_recv)

    for k in range(4):
        arrived(k, 0)
    project_both(far_in, 0, OWN_BLOCKS)
    own_pr = pltpu.make_async_copy(pr_buf, pr_ref, own_sem.at[3])
    own_pr.start()
    mig_ps = pltpu.make_async_copy(
        ps_buf.at[pl.ds(OWN_BLOCKS, MIG_BLOCKS)], ps_ref.at[pl.ds(OWN_BLOCKS, MIG_BLOCKS)],
        own_sem.at[4],
    )
    mig_ps.start()
    mig_tab = pltpu.make_async_copy(
        far_in.at[pl.ds(0, MIG_BLOCKS)], tab_ref.at[pl.ds(OWN_BLOCKS, MIG_BLOCKS)], own_sem.at[5]
    )
    mig_tab.start()
    copies = [own_tab, own_ca, own_ps, own_pr, mig_ps, mig_tab]

    for k, run in ORDER[4:]:
        at, count = RUNS[k][run]
        arrived(k, run)
        first = table_place(k, at)
        place = OWN_BLOCKS + first
        tab_copy = pltpu.make_async_copy(
            far_in.at[pl.ds(first, count)], tab_ref.at[pl.ds(place, count)], tab_sem.at[k, run]
        )
        tab_copy.start()
        blocks = jnp.concatenate([far_in[first + n] for n in range(count)], axis=1)
        out = mm(ws_t, blocks).astype(BF16)
        for n in range(count):
            ps_buf[place + n] = out[:, n * TILE : (n + 1) * TILE]
        ps_copy = pltpu.make_async_copy(
            ps_buf.at[pl.ds(place, count)], ps_ref.at[pl.ds(place, count)], ps_sem.at[k, run]
        )
        ps_copy.start()
        copies += [tab_copy, ps_copy]

    for k, run in ORDER:
        copy, exists = far_copy(out_buf, far_in, send_sem, recv_sem, k, run, 0, k ^ 1)
        guarded(exists, copy.wait_send)
    for copy in copies:
        copy.wait()


def fetch(nodes, send_rows, counts, halo_rows, send_idx, recv_idx, w_first, cot_agg):
    vmem = pl.BlockSpec(memory_space=pltpu.VMEM)
    smem = pl.BlockSpec(memory_space=pltpu.SMEM)
    hbm = pl.BlockSpec(memory_space=pl.ANY)
    dma = pltpu.SemaphoreType.DMA
    block = (TILE, TILE)
    return pl.pallas_call(
        fetch_kernel,
        name="fetch_rows",
        out_shape=(
            jax.ShapeDtypeStruct((TABLE_BLOCKS,) + block, BF16),
            jax.ShapeDtypeStruct((TABLE_BLOCKS,) + block, BF16),
            jax.ShapeDtypeStruct((OWNED_BLOCKS,) + block, BF16),
            jax.ShapeDtypeStruct((OWNED_BLOCKS,) + block, BF16),
            jax.ShapeDtypeStruct((2, TILE), jnp.int32),
        ),
        in_specs=[vmem, vmem, smem, vmem, vmem, vmem, vmem, vmem],
        out_specs=(hbm, hbm, hbm, hbm, vmem),
        scratch_shapes=[
            pltpu.VMEM((OWN_BLOCKS,) + block, BF16),
            pltpu.VMEM((FAR_BLOCKS,) + block, BF16),
            pltpu.VMEM((FAR_BLOCKS,) + block, BF16),
            pltpu.VMEM((TABLE_BLOCKS,) + block, BF16),
            pltpu.VMEM((OWNED_BLOCKS,) + block, BF16),
            pltpu.VMEM((OWNED_BLOCKS,) + block, BF16),
            dma((4, MOST_RUNS)),
            dma((4, MOST_RUNS)),
            dma((4, MOST_RUNS)),
            dma((4, MOST_RUNS)),
            dma((6,)),
        ],
        compiler_params=pltpu.CompilerParams(
            collective_id=0, has_side_effects=True, vmem_limit_bytes=VMEM_LIMIT
        ),
        cost_estimate=pl.CostEstimate(
            flops=5 * 10**9, bytes_accessed=8 * 2**20, transcendentals=0
        ),
    )(nodes, send_rows, counts, halo_rows, send_idx, recv_idx, w_first, cot_agg)


def edge_kernel(
    meta_ref, edge_ref, cot_ref, snd_ref, rcv_ref, tab_hbm, ps_t, pr_t, ca_t,
    w1_ref, w2_ref, gain_ref,
    new_ref, grad_ref, agg_ref, far_ref, own_ref, pay_ref,
    tab_ref, s_acc, ra_acc, fe_acc, w2_acc, g_acc, gain_b, w1_t, w2_t, fsr_acc, tab_sem,
):
    step = pl.program_id(0)
    steps = pl.num_programs(0)

    tab_copy = pltpu.make_async_copy(tab_hbm, tab_ref, tab_sem)

    @pl.when(step == 0)
    def _prologue():
        tab_copy.start()
        w1_t[...] = w1_ref[:TILE, :].T
        w2_t[...] = w2_ref[...].T
        gain_b[...] = jnp.broadcast_to(gain_ref[...], (TILE, TILE)).T

        def zero(b, _):
            s_acc[b] = jnp.zeros((TILE, TILE), F32)
            return 0

        lax.fori_loop(0, TABLE_BLOCKS, zero, 0, unroll=4)

        def zero_two(b, _):
            ra_acc[b] = jnp.zeros((TILE, 2 * TILE), F32)
            return 0

        lax.fori_loop(0, OWNED_BLOCKS, zero_two, 0, unroll=4)
        fe_acc[...] = jnp.zeros_like(fe_acc)
        w2_acc[...] = jnp.zeros_like(w2_acc)
        g_acc[...] = jnp.zeros_like(g_acc)

    we = w1_ref[:TILE, :]
    we_t = w1_t[...]
    w2 = w2_ref[...]
    gain = jnp.concatenate([gain_b[...]] * GROUP, axis=1)
    wide = GROUP * TILE

    def group(p, _):
        tile = (step * GROUPS + p) * GROUP
        first = pl.multiple_of(p * wide, wide)
        rows = pl.ds(first, wide)
        edges = edge_ref[rows, :]
        cot_t = cot_ref[rows, :].T.astype(F32)
        hot_s, hot_r, near, cots, blocks = [], [], [], [], []
        for side in range(GROUP):
            bs = meta_ref[0, tile + side]
            br = meta_ref[1, tile + side]
            blocks.append((bs, br))
            hs = onehot(TILE, snd_ref[pl.ds(tile + side, 1), :] & (TILE - 1), 0)
            hr = onehot(TILE, rcv_ref[pl.ds(tile + side, 1), :] & (TILE - 1), 0)
            hot_s.append(hs)
            hot_r.append(hr)
            near.append(
                mm(
                    jnp.concatenate([ps_t[bs], pr_t[br]], axis=1),
                    jnp.concatenate([hs, hr], axis=0),
                )
            )
            cots.append(mm(ca_t[br], hr))
        preact = mmt(we_t, edges) + jnp.concatenate(near, axis=1)
        sig = 0.5 * jnp.tanh(0.5 * preact) + 0.5
        hidden = preact * sig
        slope = sig + hidden * (1.0 - sig)
        hidden = hidden.astype(BF16)
        output = mm(w2_t[...], hidden)
        centred = output - jnp.sum(output, axis=0, keepdims=True) * (1.0 / TILE)
        variance = jnp.sum(centred * centred, axis=0, keepdims=True) * (1.0 / TILE)
        inverse = lax.rsqrt(variance + EPS)
        normed = centred * inverse
        message = normed * gain
        message = message.astype(BF16)
        new_ref[rows, :] = (edges.astype(F32) + message.T.astype(F32)).astype(BF16)
        d_message = cot_t + jnp.concatenate(cots, axis=1)
        weighted = d_message * normed
        g_sum = weighted[:, :TILE]
        for side in range(1, GROUP):
            g_sum += weighted[:, side * TILE : (side + 1) * TILE]
        g_acc[...] += g_sum
        d_norm = d_message * gain
        mean_one = jnp.sum(d_norm, axis=0, keepdims=True) * (1.0 / TILE)
        mean_two = jnp.sum(weighted * gain, axis=0, keepdims=True) * (1.0 / TILE)
        d_output = (inverse * (d_norm - mean_one - normed * mean_two)).astype(BF16)
        w2_acc[...] += mmt(hidden, d_output)
        d_preact = (mm(w2, d_output) * slope).astype(BF16)
        fe_acc[...] += mm(d_preact, edges)
        d_edge = mm(we, d_preact).astype(BF16)
        grad_ref[rows, :] = (cot_ref[rows, :].astype(F32) + d_edge.T.astype(F32)).astype(BF16)
        for side in range(GROUP):
            bs, br = blocks[side]
            lanes = slice(side * TILE, (side + 1) * TILE)
            d_pre = d_preact[:, lanes]
            s_acc[bs] += mmt(hot_s[side], d_pre)
            both = jnp.concatenate([d_pre, message[:, lanes]], axis=0)
            ra_acc[br] += mmt(hot_r[side], both)
        return 0

    lax.fori_loop(0, GROUPS, group, 0, unroll=UNROLL)

    @pl.when(step == steps - 1)
    def _epilogue():
        tab_copy.wait()
        ws = w1_ref[TILE : 2 * TILE, :]
        wr = w1_ref[2 * TILE :, :]
        wsr = jnp.concatenate([ws, wr], axis=1)

        fsr_acc[...] = jnp.zeros_like(fsr_acc)

        def owned(at):
            first = at * 4
            rows = pl.ds(pl.multiple_of(first * TILE, 4 * TILE), 4 * TILE)
            s = jnp.concatenate([s_acc[first + n].astype(BF16) for n in range(4)], axis=0)
            ra = [ra_acc[first + n] for n in range(4)]
            r = jnp.concatenate([x[:, :TILE].astype(BF16) for x in ra], axis=0)
            agg_ref[rows, :] = jnp.concatenate([x[:, TILE:].astype(BF16) for x in ra], axis=0)
            both = jnp.concatenate([s, r], axis=1)
            tab = jnp.concatenate([tab_ref[first + n] for n in range(4)], axis=1)
            fsr_acc[...] += mm(tab, both)
            return rows, both

        def own(at, _):
            rows, both = owned(at)
            own_ref[rows, :] = both
            return 0

        lax.fori_loop(0, OWN_BLOCKS // 4, own, 0, unroll=4)
        _, both = owned(OWN_BLOCKS // 4)
        back = mmt(wsr, both).astype(BF16)
        for n in range(MIG_BLOCKS):
            far_ref[n] = back[:, n * TILE : (n + 1) * TILE]

        def halo(at, _):
            first = OWNED_BLOCKS + at * 4
            s = jnp.concatenate([s_acc[first + n].astype(BF16) for n in range(4)], axis=0)
            back = mmt(ws, s).astype(BF16)
            for n in range(4):
                far_ref[first - OWN_BLOCKS + n] = back[:, n * TILE : (n + 1) * TILE]
            tab = jnp.concatenate([tab_ref[first + n] for n in range(4)], axis=1)
            fsr_acc[:, :TILE] += mm(tab, s)
            return 0

        lax.fori_loop(0, HALO_BLOCKS // 4, halo, 0, unroll=4)
        first = fsr_acc[:, :TILE]
        second = fsr_acc[:, TILE:]
        edge_part = fe_acc[...].T
        w2_part = w2_acc[...]
        g_row = jnp.sum(g_acc[...].T, axis=0, keepdims=True)
        g_tile = jnp.broadcast_to(g_row, (CHUNK - WEIGHT_CHUNK, TILE))
        per = TILE // WEIGHT_CHUNK
        for n, part in enumerate((edge_part, first, second, w2_part)):
            for c in range(per):
                pay_ref[n * per + c, :WEIGHT_CHUNK, :] = part[
                    c * WEIGHT_CHUNK : (c + 1) * WEIGHT_CHUNK
                ]
                pay_ref[n * per + c, WEIGHT_CHUNK:, :] = g_tile


def edge_pass(
    meta, edges, cot_edge, send_idx, recv_idx, table, ps, pr, ca, w_first, w_second, gain
):
    rows = GROUPS * GROUP * TILE
    steps = edges.shape[0] // rows
    block = (TILE, TILE)

    def whole(*shape):
        return pl.BlockSpec(shape, lambda s, m: (0,) * len(shape))

    stream = pl.BlockSpec((rows, TILE), lambda s, m: (s, 0))
    return pl.pallas_call(
        edge_kernel,
        name="edge_block",
        grid_spec=pltpu.PrefetchScalarGridSpec(
            num_scalar_prefetch=1,
            grid=(steps,),
            in_specs=[
                stream,
                stream,
                whole(*send_idx.shape),
                whole(*recv_idx.shape),
                pl.BlockSpec(memory_space=pl.ANY),
                whole(*ps.shape),
                whole(*pr.shape),
                whole(*ca.shape),
                whole(*w_first.shape),
                whole(*w_second.shape),
                whole(*gain.shape),
            ],
            out_specs=[
                stream,
                stream,
                whole(OWNED_BLOCKS * TILE, TILE),
                whole(FAR_BLOCKS, TILE, TILE),
                whole(OWN_BLOCKS * TILE, 2 * TILE),
                whole(RANKS, CHUNK, TILE),
            ],
            scratch_shapes=[
                pltpu.VMEM((TABLE_BLOCKS,) + block, BF16),
                pltpu.VMEM((TABLE_BLOCKS,) + block, F32),
                pltpu.VMEM((OWNED_BLOCKS, TILE, 2 * TILE), F32),
                pltpu.VMEM(block, F32),
                pltpu.VMEM(block, F32),
                pltpu.VMEM(block, F32),
                pltpu.VMEM(block, F32),
                pltpu.VMEM(block, BF16),
                pltpu.VMEM(block, BF16),
                pltpu.VMEM((TILE, 2 * TILE), F32),
                pltpu.SemaphoreType.DMA,
            ],
        ),
        out_shape=[
            jax.ShapeDtypeStruct(edges.shape, BF16),
            jax.ShapeDtypeStruct(edges.shape, BF16),
            jax.ShapeDtypeStruct((OWNED_BLOCKS * TILE, TILE), BF16),
            jax.ShapeDtypeStruct((FAR_BLOCKS, TILE, TILE), BF16),
            jax.ShapeDtypeStruct((OWN_BLOCKS * TILE, 2 * TILE), BF16),
            jax.ShapeDtypeStruct((RANKS, CHUNK, TILE), F32),
        ],
        compiler_params=pltpu.CompilerParams(vmem_limit_bytes=EDGE_LIMIT),
        cost_estimate=pl.CostEstimate(
            flops=12 * 10**9, bytes_accessed=24 * 2**20, transcendentals=3 * 2**20
        ),
    )(meta, edges, cot_edge, send_idx, recv_idx, table, ps, pr, ca, w_first, w_second, gain)


def rank_device(rank):
    i = lax.axis_index("gx")
    j = lax.axis_index("gy")
    gx = (rank // 8) * 4 + (lax.rem(i, 4) // 2) * 2 + lax.rem(rank, 2)
    gy = lax.rem(rank // 2, 4) * 2 + lax.rem(j, 2)
    return gx, gy


def my_rank():
    i = lax.axis_index("gx")
    j = lax.axis_index("gy")
    return (i // 4) * 8 + (j // 2) * 2 + lax.rem(i, 2)


def column_device(place):
    i = lax.axis_index("gx")
    j = lax.axis_index("gy")
    return (i // 4) * 4 + (place // 2) * 2 + lax.rem(i, 2), (j // 2) * 2 + lax.rem(place, 2)


def my_place():
    i = lax.axis_index("gx")
    j = lax.axis_index("gy")
    return (lax.rem(i, 4) // 2) * 2 + lax.rem(j, 2)


def return_kernel(
    far_ref, own_ref, pay_ref, send_ref, count_ref, halo_ref, w1_ref,
    lat_ref, sum_ref,
    back, own_buf, mine, ring, col, got, pay_sem, own_sem,
    send_sem, recv_sem, rs_send, rs_recv, col_send, col_recv, ag_send, ag_recv,
):
    rank = my_rank()
    place = my_place()
    barrier = pltpu.get_barrier_semaphore()
    greet_neighbours(barrier)

    def greet(s, _):
        device = rank_device(lax.rem(rank + s, RANKS))
        pl.semaphore_signal(barrier, inc=1, device_id=device, device_id_type=MESH)
        return 0

    lax.fori_loop(1, RANKS, greet, 0)
    for s in range(1, 4):
        device = column_device(lax.rem(place + s, 4))
        pl.semaphore_signal(barrier, inc=1, device_id=device, device_id_type=MESH)

    pay_copy = pltpu.make_async_copy(pay_ref.at[rank], ring.at[rank], pay_sem)
    pay_copy.start()
    own_copy = pltpu.make_async_copy(own_ref, own_buf, own_sem)
    own_copy.start()
    pl.semaphore_wait(barrier, neighbour_count() + RANKS - 1 + 3)

    def give(k, run, to_slot):
        return far_copy(far_ref, back, send_sem, recv_sem, k, run, 0, to_slot)

    def scatter_copy(s):
        to = lax.rem(rank + s, RANKS)
        return pltpu.make_async_remote_copy(
            src_ref=pay_ref.at[to],
            dst_ref=ring.at[rank],
            send_sem=rs_send.at[s],
            recv_sem=rs_recv.at[s],
            device_id=rank_device(to),
            device_id_type=MESH,
        )

    def start_scatter(s, _):
        scatter_copy(s).start()
        return 0

    lax.fori_loop(1, RANKS, start_scatter, 0)

    def start_give(order):
        for k, run in order:
            copy, exists = give(k, run, k ^ 1)
            guarded(exists, copy.start)

    start_give(ORDER[:X_END])

    def wait_scatter(s, _):
        scatter_copy(s).wait()
        return 0

    own_copy.wait()
    wsr = jnp.concatenate([w1_ref[TILE : 2 * TILE, :], w1_ref[2 * TILE :, :]], axis=1)

    def own_part(m, _):
        rows = pl.ds(pl.multiple_of(m * 4 * TILE, 4 * TILE), 4 * TILE)
        lat_ref[rows, :] = mmt(own_buf[rows, :], wsr)
        return 0

    lax.fori_loop(0, OWN_BLOCKS // 4, own_part, 0, unroll=2)
    lax.fori_loop(1, RANKS, wait_scatter, 0)

    pay_copy.wait()

    def add_up(s, total):
        return total + ring[s]

    col[0] = lax.fori_loop(1, RANKS, add_up, ring[0], unroll=8)

    def column_copy(s):
        return pltpu.make_async_remote_copy(
            src_ref=col.at[0],
            dst_ref=col.at[s],
            send_sem=col_send.at[s],
            recv_sem=col_recv.at[s],
            device_id=column_device(lax.rem(place + s, 4)),
            device_id_type=MESH,
        )

    for s in range(1, 4):
        column_copy(s).start()
    start_give(ORDER[X_END:])

    slot = lax.broadcasted_iota(jnp.int32, (1, TILE), 1)

    def spread(index, values_t):
        upper = jnp.broadcast_to(index >= HALF, values_t.shape)
        none = jnp.zeros((), BF16)
        right = jnp.concatenate(
            [jnp.where(upper, none, values_t), jnp.where(upper, values_t, none)], axis=0
        )
        low = jnp.where(index >= HALF, index - HALF, index)
        right = right.T

        def piece(m, _):
            first = pl.multiple_of(m * 2 * TILE, 2 * TILE)
            hot = onehot(2 * TILE, low, first)
            part = mm(hot, right)
            lat_ref[pl.ds(first, 2 * TILE), :] += part[:, :TILE]
            lat_ref[pl.ds(HALF + first, 2 * TILE), :] += part[:, TILE:]
            return 0

        lax.fori_loop(0, HALF // (2 * TILE), piece, 0, unroll=8)

    for k in range(4):
        copy, exists = give(k, 0, k)
        guarded(exists, copy.wait_recv)
        copy, exists = give(k, 0, k ^ 1)
        guarded(exists, copy.wait_send)
    indices, values = [], []
    for k in range(4):
        _, exists = neighbour(k)
        live = slot < count_ref[k]
        if exists is not None:
            live = jnp.logical_and(live, exists)
        indices.append(jnp.where(live, send_ref[pl.ds(k, 1), :], -1))
        blockv = back[k]
        if exists is not None:
            blockv = jnp.where(jnp.broadcast_to(live, (TILE, TILE)), blockv, jnp.zeros((), BF16))
        values.append(blockv)
    spread(jnp.concatenate(indices, axis=1), jnp.concatenate(values, axis=1))

    def take_all(order):
        for k, run in order:
            at, count = RUNS[k][run]
            copy, exists = give(k, run, k)

            def take(copy=copy, k=k, at=at, count=count):
                copy.wait_recv()
                first = table_place(k, at)
                index = halo_ref[pl.ds(k, 1), pl.ds((at - 1) * TILE, count * TILE)]
                spread(index, jnp.concatenate([back[first + n] for n in range(count)], axis=1))

            guarded(exists, take)

    take_all(ORDER[4:X_END])
    for s in range(1, 4):
        column_copy(s).wait()
    total = (col[0] + col[2]) + (col[1] + col[3])
    mine[...] = total[:WEIGHT_CHUNK]
    got[rank] = total[:WEIGHT_CHUNK]
    sum_ref[pl.ds(RANKS * WEIGHT_CHUNK, CHUNK - WEIGHT_CHUNK), :] = total[WEIGHT_CHUNK:]

    def gather_copy(s, owner):
        return pltpu.make_async_remote_copy(
            src_ref=mine,
            dst_ref=got.at[owner],
            send_sem=ag_send.at[s],
            recv_sem=ag_recv.at[s],
            device_id=rank_device(lax.rem(rank + s, RANKS)),
            device_id_type=MESH,
        )

    def start_gather(s, _):
        gather_copy(s, rank).start()
        return 0

    lax.fori_loop(1, RANKS, start_gather, 0)

    take_all(ORDER[X_END:])
    for k, run in ORDER[4:]:
        copy, exists = give(k, run, k ^ 1)
        guarded(exists, copy.wait_send)

    def wait_gather(s, _):
        owner = lax.rem(rank + RANKS - s, RANKS)
        gather_copy(s, owner).wait()
        return 0

    lax.fori_loop(1, RANKS, wait_gather, 0)
    for c in range(RANKS):
        sum_ref[c * WEIGHT_CHUNK : (c + 1) * WEIGHT_CHUNK, :] = got[c]


def give_back(far, own, payload, send_rows, counts, halo_rows, w_first):
    vmem = pl.BlockSpec(memory_space=pltpu.VMEM)
    smem = pl.BlockSpec(memory_space=pltpu.SMEM)
    hbm = pl.BlockSpec(memory_space=pl.ANY)
    dma = pltpu.SemaphoreType.DMA
    return pl.pallas_call(
        return_kernel,
        name="return_rows",
        out_shape=(
            jax.ShapeDtypeStruct((OWN_BLOCKS * TILE, TILE), F32),
            jax.ShapeDtypeStruct((RANKS * WEIGHT_CHUNK + CHUNK - WEIGHT_CHUNK, TILE), F32),
        ),
        in_specs=[hbm, hbm, hbm, vmem, smem, vmem, vmem],
        out_specs=(vmem, vmem),
        scratch_shapes=[
            pltpu.VMEM((FAR_BLOCKS, TILE, TILE), BF16),
            pltpu.VMEM((OWN_BLOCKS * TILE, 2 * TILE), BF16),
            pltpu.VMEM((WEIGHT_CHUNK, TILE), F32),
            pltpu.VMEM((RANKS, CHUNK, TILE), F32),
            pltpu.VMEM((4, CHUNK, TILE), F32),
            pltpu.VMEM((RANKS, WEIGHT_CHUNK, TILE), F32),
            dma,
            dma,
            dma((4, MOST_RUNS)),
            dma((4, MOST_RUNS)),
            dma((RANKS,)),
            dma((RANKS,)),
            dma((4,)),
            dma((4,)),
            dma((RANKS,)),
            dma((RANKS,)),
        ],
        compiler_params=pltpu.CompilerParams(
            collective_id=1, has_side_effects=True, vmem_limit_bytes=RETURN_LIMIT
        ),
        cost_estimate=pl.CostEstimate(
            flops=5 * 10**9, bytes_accessed=8 * 2**20, transcendentals=0
        ),
    )(far, own, payload, send_rows, counts, halo_rows, w_first)


def per_device(
    latent,
    edge_state,
    w_first,
    w_second,
    norm_gain,
    send_list,
    send_count,
    halo_list,
    senders,
    receivers,
    cotangent_edge,
    cotangent_agg,
):
    send_rows = send_list[0, 0]
    halo_rows = halo_list[0, 0]
    counts = send_count[0, 0]
    send_idx = senders.reshape(-1, TILE)
    recv_idx = receivers.reshape(-1, TILE)
    table, ps, pr, ca, meta = fetch(
        latent[0, 0], send_rows, counts, halo_rows, send_idx, recv_idx, w_first, cotangent_agg[0, 0]
    )
    new_edge, grad_edge, aggregate, far, own, payload = edge_pass(
        meta,
        edge_state[0, 0],
        cotangent_edge[0, 0],
        send_idx,
        recv_idx,
        table,
        ps,
        pr,
        ca,
        w_first,
        w_second,
        norm_gain.reshape(1, TILE),
    )
    grad_latent, sums = give_back(far, own, payload, send_rows, counts, halo_rows, w_first)
    return (
        new_edge[None, None],
        aggregate[None, None],
        grad_edge[None, None],
        grad_latent[None, None],
        sums[: 3 * TILE],
        sums[3 * TILE : 4 * TILE],
        sums[4 * TILE],
    )


def solution(mesh):
    rows = P("gx", "gy", None, None)
    flat = P("gx", "gy", None)
    in_specs = (rows, rows, P(), P(), P(), rows, flat, rows, flat, flat, rows, rows)
    out_specs = (rows, rows, rows, rows, P(), P(), P())
    return jax.shard_map(
        per_device, mesh=mesh, in_specs=in_specs, out_specs=out_specs, check_vma=False
    )
```

```python
import functools

import jax
import jax.numpy as jnp
from jax import lax
from jax.experimental import pallas as pl
from jax.experimental.pallas import tpu as pltpu
from jax.sharding import PartitionSpec as P

MESH = pl.DeviceIdType.MESH
F32 = jnp.float32
BF16 = jnp.bfloat16
TILE = 128
EPS = 1e-05
N_GX = 16
N_GY = 8
OWN_BLOCKS = 32
MIG_BLOCKS = 4
HALO_BLOCKS = 32
OWNED_BLOCKS = OWN_BLOCKS + MIG_BLOCKS
FAR_BLOCKS = MIG_BLOCKS + HALO_BLOCKS
TABLE_BLOCKS = OWN_BLOCKS + FAR_BLOCKS
PER_DIR = HALO_BLOCKS // 4
HALF = OWN_BLOCKS * TILE // 2
GROUP = 16
GROUPS = 1
UNROLL = 1
RANKS = 32
CHUNK = 24
VMEM_LIMIT = 62 * 2**20
RETURN_LIMIT = 24 * 2**20
EDGE_LIMIT = 48 * 2**20
WEIGHT_CHUNK = 16


def mm(a, b):
    return jnp.dot(a, b, preferred_element_type=F32)


def mmt(a, b):
    return lax.dot_general(a, b, (((1,), (1,)), ((), ())), preferred_element_type=F32)


def onehot(rows, row_index, base):
    lanes = row_index.shape[1]
    row = lax.broadcasted_iota(jnp.int16, (rows, lanes), 0)
    index = jnp.broadcast_to((row_index - base).astype(jnp.int16), (rows, lanes))
    return jnp.where(row == index, jnp.ones((), BF16), jnp.zeros((), BF16))


def neighbour(k):
    i = lax.axis_index("gx")
    j = lax.axis_index("gy")
    if k == 0:
        return (lax.rem(i + N_GX - 1, N_GX), j), None
    if k == 1:
        return (lax.rem(i + 1, N_GX), j), None
    if k == 2:
        return (i, j - 1), j > 0
    return (i, j + 1), j < N_GY - 1


def guarded(exists, action):
    if exists is None:
        action()
    else:
        pl.when(exists)(action)


def greet_neighbours(barrier):
    for k in range(4):
        device, exists = neighbour(k)

        def signal(device=device):
            pl.semaphore_signal(barrier, inc=1, device_id=device, device_id_type=MESH)

        guarded(exists, signal)


def neighbour_count():
    j = lax.axis_index("gy")
    return 2 + jnp.where(j > 0, 1, 0) + jnp.where(j < N_GY - 1, 1, 0)


X_RUNS = ((0, 1), (1, 4), (5, 4))
Y_RUNS = ((0, 1), (1, 4), (5, 2), (7, 2))
RUNS = (X_RUNS, X_RUNS, Y_RUNS, Y_RUNS)
MOST_RUNS = 4
LONGEST = 4
ORDER = (
    [(k, 0) for k in (2, 3, 0, 1)]
    + [(k, run) for run in (1, 2) for k in (0, 1)]
    + [(k, run) for run in (1, 2, 3) for k in (2, 3)]
)
X_END = 4 + 4


def table_place(direction, at):
    if at == 0:
        return direction
    return MIG_BLOCKS + direction * PER_DIR + at - 1


def far_copy(src, dst, send_sem, recv_sem, k, run, base, to_slot):
    at, count = RUNS[k][run]
    device, exists = neighbour(k)
    copy = pltpu.make_async_remote_copy(
        src_ref=src.at[pl.ds(table_place(k, at), count)],
        dst_ref=dst.at[pl.ds(base + table_place(to_slot, at), count)],
        send_sem=send_sem.at[k, run],
        recv_sem=recv_sem.at[to_slot, run],
        device_id=device,
        device_id_type=MESH,
    )
    return copy, exists


def fetch_kernel(
    lat_ref, send_ref, count_ref, halo_ref, snd_ref, rcv_ref, w1_ref, cota_ref,
    tab_ref, ps_ref, pr_ref, ca_ref, meta_ref,
    lat_t, out_buf, far_in, ps_buf, pr_buf, ca_buf,
    send_sem, recv_sem, tab_sem, ps_sem, own_sem,
):
    barrier = pltpu.get_barrier_semaphore()
    greet_neighbours(barrier)

    def turn(b, _):
        rows = lat_ref[pl.ds(pl.multiple_of(b * TILE, TILE), TILE), :]
        lat_t[b] = rows.T
        return 0

    lax.fori_loop(0, OWN_BLOCKS, turn, 0, unroll=8)
    own_tab = pltpu.make_async_copy(lat_t, tab_ref.at[pl.ds(0, OWN_BLOCKS)], own_sem.at[0])
    own_tab.start()
    half = OWN_BLOCKS // 2

    def pick(index):
        low = jnp.where(index >= HALF, index - HALF, index)
        acc = None
        for piece in range(half // 2):
            hot = onehot(2 * TILE, low, piece * 2 * TILE)
            left = jnp.concatenate(
                [
                    jnp.concatenate([lat_t[2 * piece], lat_t[2 * piece + 1]], axis=1),
                    jnp.concatenate([lat_t[half + 2 * piece], lat_t[half + 2 * piece + 1]], axis=1),
                ],
                axis=0,
            )
            part = mm(left, hot)
            acc = part if acc is None else acc + part
        upper = jnp.broadcast_to(index >= HALF, (TILE, index.shape[1]))
        return jnp.where(upper, acc[TILE:], acc[:TILE]).astype(BF16)

    slot = lax.broadcasted_iota(jnp.int32, (1, TILE), 1)

    def live_index(k):
        return jnp.where(slot < count_ref[k], send_ref[pl.ds(k, 1), :], -1)

    for pair in range(2):
        index = jnp.concatenate([live_index(2 * pair), live_index(2 * pair + 1)], axis=1)
        rows = pick(index)
        out_buf[2 * pair] = rows[:, :TILE]
        out_buf[2 * pair + 1] = rows[:, TILE:]

    pl.semaphore_wait(barrier, neighbour_count())

    for k, run in ORDER:
        at, count = RUNS[k][run]
        if at:

            def gather(step, _, k=k, at=at):
                first = pl.multiple_of((at - 1) * TILE + step * 2 * TILE, 2 * TILE)
                rows = pick(halo_ref[pl.ds(k, 1), pl.ds(first, 2 * TILE)])
                place = table_place(k, at) + 2 * step
                out_buf[place] = rows[:, :TILE]
                out_buf[place + 1] = rows[:, TILE:]
                return 0

            lax.fori_loop(0, count // 2, gather, 0)
        copy, exists = far_copy(out_buf, far_in, send_sem, recv_sem, k, run, 0, k ^ 1)
        guarded(exists, copy.start)

    for k in (2, 3):
        _, exists = neighbour(k)

        def fill(k=k):
            for at, count in RUNS[k]:
                first = table_place(k, at)
                far_in[first : first + count] = jnp.zeros((count, TILE, TILE), BF16)

        pl.when(jnp.logical_not(exists))(fill)

    firsts = lax.shift_right_logical(
        jnp.concatenate([snd_ref[...].T[:1], rcv_ref[...].T[:1]], axis=0), 7
    )
    meta_ref[...] = firsts
    ws_t = w1_ref[TILE : 2 * TILE, :].T
    both_t = jnp.concatenate([ws_t, w1_ref[2 * TILE :, :].T], axis=0)

    def turn_cotangents(at, _):
        first = at * 4
        rows = pl.ds(pl.multiple_of(first * TILE, 4 * TILE), 4 * TILE)
        turned = cota_ref[rows, :].T
        for n in range(4):
            ca_buf[first + n] = turned[:, n * TILE : (n + 1) * TILE]
        return 0

    lax.fori_loop(0, OWNED_BLOCKS // 4, turn_cotangents, 0)
    own_ca = pltpu.make_async_copy(ca_buf, ca_ref, own_sem.at[1])
    own_ca.start()

    def project_both(source, first, place):
        blocks = jnp.concatenate([source[first + n] for n in range(4)], axis=1)
        out = mm(both_t, blocks).astype(BF16)
        for n in range(4):
            ps_buf[place + n] = out[:TILE, n * TILE : (n + 1) * TILE]
            pr_buf[place + n] = out[TILE:, n * TILE : (n + 1) * TILE]

    def project_own(at, _):
        project_both(lat_t, at * 4, at * 4)
        return 0

    lax.fori_loop(0, OWN_BLOCKS // 4, project_own, 0)
    own_ps = pltpu.make_async_copy(
        ps_buf.at[pl.ds(0, OWN_BLOCKS)], ps_ref.at[pl.ds(0, OWN_BLOCKS)], own_sem.at[2]
    )
    own_ps.start()

    def arrived(k, run):
        copy, exists = far_copy(out_buf, far_in, send_sem, recv_sem, k, run, 0, k)
        guarded(exists, copy.wait_recv)

    for k in range(4):
        arrived(k, 0)
    project_both(far_in, 0, OWN_BLOCKS)
    own_pr = pltpu.make_async_copy(pr_buf, pr_ref, own_sem.at[3])
    own_pr.start()
    mig_ps = pltpu.make_async_copy(
        ps_buf.at[pl.ds(OWN_BLOCKS, MIG_BLOCKS)], ps_ref.at[pl.ds(OWN_BLOCKS, MIG_BLOCKS)],
        own_sem.at[4],
    )
    mig_ps.start()
    mig_tab = pltpu.make_async_copy(
        far_in.at[pl.ds(0, MIG_BLOCKS)], tab_ref.at[pl.ds(OWN_BLOCKS, MIG_BLOCKS)], own_sem.at[5]
    )
    mig_tab.start()
    copies = [own_tab, own_ca, own_ps, own_pr, mig_ps, mig_tab]

    for k, run in ORDER[4:]:
        at, count = RUNS[k][run]
        arrived(k, run)
        first = table_place(k, at)
        place = OWN_BLOCKS + first
        tab_copy = pltpu.make_async_copy(
            far_in.at[pl.ds(first, count)], tab_ref.at[pl.ds(place, count)], tab_sem.at[k, run]
        )
        tab_copy.start()
        blocks = jnp.concatenate([far_in[first + n] for n in range(count)], axis=1)
        out = mm(ws_t, blocks).astype(BF16)
        for n in range(count):
            ps_buf[place + n] = out[:, n * TILE : (n + 1) * TILE]
        ps_copy = pltpu.make_async_copy(
            ps_buf.at[pl.ds(place, count)], ps_ref.at[pl.ds(place, count)], ps_sem.at[k, run]
        )
        ps_copy.start()
        copies += [tab_copy, ps_copy]

    for k, run in ORDER:
        copy, exists = far_copy(out_buf, far_in, send_sem, recv_sem, k, run, 0, k ^ 1)
        guarded(exists, copy.wait_send)
    for copy in copies:
        copy.wait()


def fetch(nodes, send_rows, counts, halo_rows, send_idx, recv_idx, w_first, cot_agg):
    vmem = pl.BlockSpec(memory_space=pltpu.VMEM)
    smem = pl.BlockSpec(memory_space=pltpu.SMEM)
    hbm = pl.BlockSpec(memory_space=pl.ANY)
    dma = pltpu.SemaphoreType.DMA
    block = (TILE, TILE)
    return pl.pallas_call(
        fetch_kernel,
        name="fetch_rows",
        out_shape=(
            jax.ShapeDtypeStruct((TABLE_BLOCKS,) + block, BF16),
            jax.ShapeDtypeStruct((TABLE_BLOCKS,) + block, BF16),
            jax.ShapeDtypeStruct((OWNED_BLOCKS,) + block, BF16),
            jax.ShapeDtypeStruct((OWNED_BLOCKS,) + block, BF16),
            jax.ShapeDtypeStruct((2, TILE), jnp.int32),
        ),
        in_specs=[vmem, vmem, smem, vmem, vmem, vmem, vmem, vmem],
        out_specs=(hbm, hbm, hbm, hbm, vmem),
        scratch_shapes=[
            pltpu.VMEM((OWN_BLOCKS,) + block, BF16),
            pltpu.VMEM((FAR_BLOCKS,) + block, BF16),
            pltpu.VMEM((FAR_BLOCKS,) + block, BF16),
            pltpu.VMEM((TABLE_BLOCKS,) + block, BF16),
            pltpu.VMEM((OWNED_BLOCKS,) + block, BF16),
            pltpu.VMEM((OWNED_BLOCKS,) + block, BF16),
            dma((4, MOST_RUNS)),
            dma((4, MOST_RUNS)),
            dma((4, MOST_RUNS)),
            dma((4, MOST_RUNS)),
            dma((6,)),
        ],
        compiler_params=pltpu.CompilerParams(
            collective_id=0, has_side_effects=True, vmem_limit_bytes=VMEM_LIMIT
        ),
        cost_estimate=pl.CostEstimate(
            flops=5 * 10**9, bytes_accessed=8 * 2**20, transcendentals=0
        ),
    )(nodes, send_rows, counts, halo_rows, send_idx, recv_idx, w_first, cot_agg)


def edge_kernel(
    meta_ref, edge_ref, cot_ref, snd_ref, rcv_ref, tab_hbm, ps_t, pr_t, ca_t,
    w1_ref, w2_ref, gain_ref,
    new_ref, grad_ref, agg_ref, far_ref, own_ref, pay_ref,
    tab_ref, s_acc, ra_acc, fe_acc, w2_acc, g_acc, gain_b, w1_t, w2_t, fsr_acc, tab_sem,
):
    step = pl.program_id(0)
    steps = pl.num_programs(0)

    tab_copy = pltpu.make_async_copy(tab_hbm, tab_ref, tab_sem)

    @pl.when(step == 0)
    def _prologue():
        tab_copy.start()
        w1_t[...] = w1_ref[:TILE, :].T
        w2_t[...] = w2_ref[...].T
        gain_b[...] = jnp.broadcast_to(gain_ref[...], (TILE, TILE)).T

        def zero(b, _):
            s_acc[b] = jnp.zeros((TILE, TILE), F32)
            return 0

        lax.fori_loop(0, TABLE_BLOCKS, zero, 0, unroll=4)

        def zero_two(b, _):
            ra_acc[b] = jnp.zeros((TILE, 2 * TILE), F32)
            return 0

        lax.fori_loop(0, OWNED_BLOCKS, zero_two, 0, unroll=4)
        fe_acc[...] = jnp.zeros_like(fe_acc)
        w2_acc[...] = jnp.zeros_like(w2_acc)
        g_acc[...] = jnp.zeros_like(g_acc)

    we = w1_ref[:TILE, :]
    we_t = w1_t[...]
    w2 = w2_ref[...]
    gain = jnp.concatenate([gain_b[...]] * GROUP, axis=1)
    wide = GROUP * TILE

    def group(p, _):
        tile = (step * GROUPS + p) * GROUP
        first = pl.multiple_of(p * wide, wide)
        rows = pl.ds(first, wide)
        edges = edge_ref[rows, :]
        cot_t = cot_ref[rows, :].T.astype(F32)
        hot_s, hot_r, near, cots, blocks = [], [], [], [], []
        for side in range(GROUP):
            bs = meta_ref[0, tile + side]
            br = meta_ref[1, tile + side]
            blocks.append((bs, br))
            hs = onehot(TILE, snd_ref[pl.ds(tile + side, 1), :] & (TILE - 1), 0)
            hr = onehot(TILE, rcv_ref[pl.ds(tile + side, 1), :] & (TILE - 1), 0)
            hot_s.append(hs)
            hot_r.append(hr)
            near.append(
                mm(
                    jnp.concatenate([ps_t[bs], pr_t[br]], axis=1),
                    jnp.concatenate([hs, hr], axis=0),
                )
            )
            cots.append(mm(ca_t[br], hr))
        preact = mmt(we_t, edges) + jnp.concatenate(near, axis=1)
        sig = 0.5 * jnp.tanh(0.5 * preact) + 0.5
        hidden = preact * sig
        slope = sig + hidden * (1.0 - sig)
        hidden = hidden.astype(BF16)
        output = mm(w2_t[...], hidden)
        centred = output - jnp.sum(output, axis=0, keepdims=True) * (1.0 / TILE)
        variance = jnp.sum(centred * centred, axis=0, keepdims=True) * (1.0 / TILE)
        inverse = lax.rsqrt(variance + EPS)
        normed = centred * inverse
        message = normed * gain
        message = message.astype(BF16)
        new_ref[rows, :] = (edges.astype(F32) + message.T.astype(F32)).astype(BF16)
        d_message = cot_t + jnp.concatenate(cots, axis=1)
        weighted = d_message * normed
        g_sum = weighted[:, :TILE]
        for side in range(1, GROUP):
            g_sum += weighted[:, side * TILE : (side + 1) * TILE]
        g_acc[...] += g_sum
        d_norm = d_message * gain
        mean_one = jnp.sum(d_norm, axis=0, keepdims=True) * (1.0 / TILE)
        mean_two = jnp.sum(weighted * gain, axis=0, keepdims=True) * (1.0 / TILE)
        d_output = (inverse * (d_norm - mean_one - normed * mean_two)).astype(BF16)
        w2_acc[...] += mmt(hidden, d_output)
        d_preact = (mm(w2, d_output) * slope).astype(BF16)
        fe_acc[...] += mm(d_preact, edges)
        d_edge = mm(we, d_preact).astype(BF16)
        grad_ref[rows, :] = (cot_ref[rows, :].astype(F32) + d_edge.T.astype(F32)).astype(BF16)
        for side in range(GROUP):
            bs, br = blocks[side]
            lanes = slice(side * TILE, (side + 1) * TILE)
            d_pre = d_preact[:, lanes]
            s_acc[bs] += mmt(hot_s[side], d_pre)
            both = jnp.concatenate([d_pre, message[:, lanes]], axis=0)
            ra_acc[br] += mmt(hot_r[side], both)
        return 0

    lax.fori_loop(0, GROUPS, group, 0, unroll=UNROLL)

    @pl.when(step == steps - 1)
    def _epilogue():
        tab_copy.wait()
        ws = w1_ref[TILE : 2 * TILE, :]
        wr = w1_ref[2 * TILE :, :]
        wsr = jnp.concatenate([ws, wr], axis=1)

        fsr_acc[...] = jnp.zeros_like(fsr_acc)

        def owned(at):
            first = at * 4
            rows = pl.ds(pl.multiple_of(first * TILE, 4 * TILE), 4 * TILE)
            s = jnp.concatenate([s_acc[first + n].astype(BF16) for n in range(4)], axis=0)
            ra = [ra_acc[first + n] for n in range(4)]
            r = jnp.concatenate([x[:, :TILE].astype(BF16) for x in ra], axis=0)
            agg_ref[rows, :] = jnp.concatenate([x[:, TILE:].astype(BF16) for x in ra], axis=0)
            both = jnp.concatenate([s, r], axis=1)
            tab = jnp.concatenate([tab_ref[first + n] for n in range(4)], axis=1)
            fsr_acc[...] += mm(tab, both)
            return rows, both

        def own(at, _):
            rows, both = owned(at)
            own_ref[rows, :] = both
            return 0

        lax.fori_loop(0, OWN_BLOCKS // 4, own, 0, unroll=8)
        _, both = owned(OWN_BLOCKS // 4)
        back = mmt(wsr, both).astype(BF16)
        for n in range(MIG_BLOCKS):
            far_ref[n] = back[:, n * TILE : (n + 1) * TILE]

        def halo(at, _):
            first = OWNED_BLOCKS + at * 4
            s = jnp.concatenate([s_acc[first + n].astype(BF16) for n in range(4)], axis=0)
            back = mmt(ws, s).astype(BF16)
            for n in range(4):
                far_ref[first - OWN_BLOCKS + n] = back[:, n * TILE : (n + 1) * TILE]
            tab = jnp.concatenate([tab_ref[first + n] for n in range(4)], axis=1)
            fsr_acc[:, :TILE] += mm(tab, s)
            return 0

        lax.fori_loop(0, HALO_BLOCKS // 4, halo, 0, unroll=8)
        first = fsr_acc[:, :TILE]
        second = fsr_acc[:, TILE:]
        edge_part = fe_acc[...].T
        w2_part = w2_acc[...]
        g_row = jnp.sum(g_acc[...].T, axis=0, keepdims=True)
        g_tile = jnp.broadcast_to(g_row, (CHUNK - WEIGHT_CHUNK, TILE))
        per = TILE // WEIGHT_CHUNK
        for n, part in enumerate((edge_part, first, second, w2_part)):
            for c in range(per):
                pay_ref[n * per + c, :WEIGHT_CHUNK, :] = part[
                    c * WEIGHT_CHUNK : (c + 1) * WEIGHT_CHUNK
                ]
                pay_ref[n * per + c, WEIGHT_CHUNK:, :] = g_tile


def edge_pass(
    meta, edges, cot_edge, send_idx, recv_idx, table, ps, pr, ca, w_first, w_second, gain
):
    rows = GROUPS * GROUP * TILE
    steps = edges.shape[0] // rows
    block = (TILE, TILE)

    def whole(*shape):
        return pl.BlockSpec(shape, lambda s, m: (0,) * len(shape))

    stream = pl.BlockSpec((rows, TILE), lambda s, m: (s, 0))
    return pl.pallas_call(
        edge_kernel,
        name="edge_block",
        grid_spec=pltpu.PrefetchScalarGridSpec(
            num_scalar_prefetch=1,
            grid=(steps,),
            in_specs=[
                stream,
                stream,
                whole(*send_idx.shape),
                whole(*recv_idx.shape),
                pl.BlockSpec(memory_space=pl.ANY),
                whole(*ps.shape),
                whole(*pr.shape),
                whole(*ca.shape),
                whole(*w_first.shape),
                whole(*w_second.shape),
                whole(*gain.shape),
            ],
            out_specs=[
                stream,
                stream,
                whole(OWNED_BLOCKS * TILE, TILE),
                whole(FAR_BLOCKS, TILE, TILE),
                whole(OWN_BLOCKS * TILE, 2 * TILE),
                whole(RANKS, CHUNK, TILE),
            ],
            scratch_shapes=[
                pltpu.VMEM((TABLE_BLOCKS,) + block, BF16),
                pltpu.VMEM((TABLE_BLOCKS,) + block, F32),
                pltpu.VMEM((OWNED_BLOCKS, TILE, 2 * TILE), F32),
                pltpu.VMEM(block, F32),
                pltpu.VMEM(block, F32),
                pltpu.VMEM(block, F32),
                pltpu.VMEM(block, F32),
                pltpu.VMEM(block, BF16),
                pltpu.VMEM(block, BF16),
                pltpu.VMEM((TILE, 2 * TILE), F32),
                pltpu.SemaphoreType.DMA,
            ],
        ),
        out_shape=[
            jax.ShapeDtypeStruct(edges.shape, BF16),
            jax.ShapeDtypeStruct(edges.shape, BF16),
            jax.ShapeDtypeStruct((OWNED_BLOCKS * TILE, TILE), BF16),
            jax.ShapeDtypeStruct((FAR_BLOCKS, TILE, TILE), BF16),
            jax.ShapeDtypeStruct((OWN_BLOCKS * TILE, 2 * TILE), BF16),
            jax.ShapeDtypeStruct((RANKS, CHUNK, TILE), F32),
        ],
        compiler_params=pltpu.CompilerParams(vmem_limit_bytes=EDGE_LIMIT),
        cost_estimate=pl.CostEstimate(
            flops=12 * 10**9, bytes_accessed=24 * 2**20, transcendentals=3 * 2**20
        ),
    )(meta, edges, cot_edge, send_idx, recv_idx, table, ps, pr, ca, w_first, w_second, gain)


def rank_device(rank):
    i = lax.axis_index("gx")
    j = lax.axis_index("gy")
    gx = (rank // 8) * 4 + (lax.rem(i, 4) // 2) * 2 + lax.rem(rank, 2)
    gy = lax.rem(rank // 2, 4) * 2 + lax.rem(j, 2)
    return gx, gy


def my_rank():
    i = lax.axis_index("gx")
    j = lax.axis_index("gy")
    return (i // 4) * 8 + (j // 2) * 2 + lax.rem(i, 2)


def column_device(place):
    i = lax.axis_index("gx")
    j = lax.axis_index("gy")
    return (i // 4) * 4 + (place // 2) * 2 + lax.rem(i, 2), (j // 2) * 2 + lax.rem(place, 2)


def my_place():
    i = lax.axis_index("gx")
    j = lax.axis_index("gy")
    return (lax.rem(i, 4) // 2) * 2 + lax.rem(j, 2)


def return_kernel(
    far_ref, own_ref, pay_ref, send_ref, count_ref, halo_ref, w1_ref,
    lat_ref, sum_ref,
    back, own_buf, mine, ring, col, got, pay_sem, own_sem,
    send_sem, recv_sem, rs_send, rs_recv, col_send, col_recv, ag_send, ag_recv,
):
    rank = my_rank()
    place = my_place()
    barrier = pltpu.get_barrier_semaphore()
    greet_neighbours(barrier)

    def greet(s, _):
        device = rank_device(lax.rem(rank + s, RANKS))
        pl.semaphore_signal(barrier, inc=1, device_id=device, device_id_type=MESH)
        return 0

    lax.fori_loop(1, RANKS, greet, 0)
    for s in range(1, 4):
        device = column_device(lax.rem(place + s, 4))
        pl.semaphore_signal(barrier, inc=1, device_id=device, device_id_type=MESH)

    pay_copy = pltpu.make_async_copy(pay_ref.at[rank], ring.at[rank], pay_sem)
    pay_copy.start()
    own_copy = pltpu.make_async_copy(own_ref, own_buf, own_sem)
    own_copy.start()
    pl.semaphore_wait(barrier, neighbour_count() + RANKS - 1 + 3)

    def give(k, run, to_slot):
        return far_copy(far_ref, back, send_sem, recv_sem, k, run, 0, to_slot)

    def scatter_copy(s):
        to = lax.rem(rank + s, RANKS)
        return pltpu.make_async_remote_copy(
            src_ref=pay_ref.at[to],
            dst_ref=ring.at[rank],
            send_sem=rs_send.at[s],
            recv_sem=rs_recv.at[s],
            device_id=rank_device(to),
            device_id_type=MESH,
        )

    def start_scatter(s, _):
        scatter_copy(s).start()
        return 0

    lax.fori_loop(1, RANKS, start_scatter, 0)

    def start_give(order):
        for k, run in order:
            copy, exists = give(k, run, k ^ 1)
            guarded(exists, copy.start)

    start_give(ORDER[:X_END])

    def wait_scatter(s, _):
        scatter_copy(s).wait()
        return 0

    own_copy.wait()
    wsr = jnp.concatenate([w1_ref[TILE : 2 * TILE, :], w1_ref[2 * TILE :, :]], axis=1)

    def own_part(m, _):
        rows = pl.ds(pl.multiple_of(m * 4 * TILE, 4 * TILE), 4 * TILE)
        lat_ref[rows, :] = mmt(own_buf[rows, :], wsr)
        return 0

    lax.fori_loop(0, OWN_BLOCKS // 4, own_part, 0, unroll=8)
    lax.fori_loop(1, RANKS, wait_scatter, 0)

    pay_copy.wait()

    def add_up(s, total):
        return total + ring[s]

    col[0] = lax.fori_loop(1, RANKS, add_up, ring[0], unroll=8)

    def column_copy(s):
        return pltpu.make_async_remote_copy(
            src_ref=col.at[0],
            dst_ref=col.at[s],
            send_sem=col_send.at[s],
            recv_sem=col_recv.at[s],
            device_id=column_device(lax.rem(place + s, 4)),
            device_id_type=MESH,
        )

    for s in range(1, 4):
        column_copy(s).start()
    start_give(ORDER[X_END:])

    slot = lax.broadcasted_iota(jnp.int32, (1, TILE), 1)

    def spread(index, values_t):
        upper = jnp.broadcast_to(index >= HALF, values_t.shape)
        none = jnp.zeros((), BF16)
        right = jnp.concatenate(
            [jnp.where(upper, none, values_t), jnp.where(upper, values_t, none)], axis=0
        )
        low = jnp.where(index >= HALF, index - HALF, index)
        right = right.T

        def piece(m, _):
            first = pl.multiple_of(m * 2 * TILE, 2 * TILE)
            hot = onehot(2 * TILE, low, first)
            part = mm(hot, right)
            lat_ref[pl.ds(first, 2 * TILE), :] += part[:, :TILE]
            lat_ref[pl.ds(HALF + first, 2 * TILE), :] += part[:, TILE:]
            return 0

        lax.fori_loop(0, HALF // (2 * TILE), piece, 0, unroll=8)

    for k in range(4):
        copy, exists = give(k, 0, k)
        guarded(exists, copy.wait_recv)
        copy, exists = give(k, 0, k ^ 1)
        guarded(exists, copy.wait_send)
    indices, values = [], []
    for k in range(4):
        _, exists = neighbour(k)
        live = slot < count_ref[k]
        if exists is not None:
            live = jnp.logical_and(live, exists)
        indices.append(jnp.where(live, send_ref[pl.ds(k, 1), :], -1))
        blockv = back[k]
        if exists is not None:
            blockv = jnp.where(jnp.broadcast_to(live, (TILE, TILE)), blockv, jnp.zeros((), BF16))
        values.append(blockv)
    spread(jnp.concatenate(indices, axis=1), jnp.concatenate(values, axis=1))

    def take_all(order):
        for k, run in order:
            at, count = RUNS[k][run]
            copy, exists = give(k, run, k)

            def take(copy=copy, k=k, at=at, count=count):
                copy.wait_recv()
                first = table_place(k, at)
                index = halo_ref[pl.ds(k, 1), pl.ds((at - 1) * TILE, count * TILE)]
                spread(index, jnp.concatenate([back[first + n] for n in range(count)], axis=1))

            guarded(exists, take)

    take_all(ORDER[4:X_END])
    for s in range(1, 4):
        column_copy(s).wait()
    total = (col[0] + col[2]) + (col[1] + col[3])
    mine[...] = total[:WEIGHT_CHUNK]
    got[rank] = total[:WEIGHT_CHUNK]
    sum_ref[pl.ds(RANKS * WEIGHT_CHUNK, CHUNK - WEIGHT_CHUNK), :] = total[WEIGHT_CHUNK:]

    def gather_copy(s, owner):
        return pltpu.make_async_remote_copy(
            src_ref=mine,
            dst_ref=got.at[owner],
            send_sem=ag_send.at[s],
            recv_sem=ag_recv.at[s],
            device_id=rank_device(lax.rem(rank + s, RANKS)),
            device_id_type=MESH,
        )

    def start_gather(s, _):
        gather_copy(s, rank).start()
        return 0

    lax.fori_loop(1, RANKS, start_gather, 0)

    take_all(ORDER[X_END:])
    for k, run in ORDER[4:]:
        copy, exists = give(k, run, k ^ 1)
        guarded(exists, copy.wait_send)

    def wait_gather(s, _):
        owner = lax.rem(rank + RANKS - s, RANKS)
        gather_copy(s, owner).wait()
        return 0

    lax.fori_loop(1, RANKS, wait_gather, 0)
    for c in range(RANKS):
        sum_ref[c * WEIGHT_CHUNK : (c + 1) * WEIGHT_CHUNK, :] = got[c]


def give_back(far, own, payload, send_rows, counts, halo_rows, w_first):
    vmem = pl.BlockSpec(memory_space=pltpu.VMEM)
    smem = pl.BlockSpec(memory_space=pltpu.SMEM)
    hbm = pl.BlockSpec(memory_space=pl.ANY)
    dma = pltpu.SemaphoreType.DMA
    return pl.pallas_call(
        return_kernel,
        name="return_rows",
        out_shape=(
            jax.ShapeDtypeStruct((OWN_BLOCKS * TILE, TILE), F32),
            jax.ShapeDtypeStruct((RANKS * WEIGHT_CHUNK + CHUNK - WEIGHT_CHUNK, TILE), F32),
        ),
        in_specs=[hbm, hbm, hbm, vmem, smem, vmem, vmem],
        out_specs=(vmem, vmem),
        scratch_shapes=[
            pltpu.VMEM((FAR_BLOCKS, TILE, TILE), BF16),
            pltpu.VMEM((OWN_BLOCKS * TILE, 2 * TILE), BF16),
            pltpu.VMEM((WEIGHT_CHUNK, TILE), F32),
            pltpu.VMEM((RANKS, CHUNK, TILE), F32),
            pltpu.VMEM((4, CHUNK, TILE), F32),
            pltpu.VMEM((RANKS, WEIGHT_CHUNK, TILE), F32),
            dma,
            dma,
            dma((4, MOST_RUNS)),
            dma((4, MOST_RUNS)),
            dma((RANKS,)),
            dma((RANKS,)),
            dma((4,)),
            dma((4,)),
            dma((RANKS,)),
            dma((RANKS,)),
        ],
        compiler_params=pltpu.CompilerParams(
            collective_id=1, has_side_effects=True, vmem_limit_bytes=RETURN_LIMIT
        ),
        cost_estimate=pl.CostEstimate(
            flops=5 * 10**9, bytes_accessed=8 * 2**20, transcendentals=0
        ),
    )(far, own, payload, send_rows, counts, halo_rows, w_first)


def per_device(
    latent,
    edge_state,
    w_first,
    w_second,
    norm_gain,
    send_list,
    send_count,
    halo_list,
    senders,
    receivers,
    cotangent_edge,
    cotangent_agg,
):
    send_rows = send_list[0, 0]
    halo_rows = halo_list[0, 0]
    counts = send_count[0, 0]
    send_idx = senders.reshape(-1, TILE)
    recv_idx = receivers.reshape(-1, TILE)
    table, ps, pr, ca, meta = fetch(
        latent[0, 0], send_rows, counts, halo_rows, send_idx, recv_idx, w_first, cotangent_agg[0, 0]
    )
    new_edge, grad_edge, aggregate, far, own, payload = edge_pass(
        meta,
        edge_state[0, 0],
        cotangent_edge[0, 0],
        send_idx,
        recv_idx,
        table,
        ps,
        pr,
        ca,
        w_first,
        w_second,
        norm_gain.reshape(1, TILE),
    )
    grad_latent, sums = give_back(far, own, payload, send_rows, counts, halo_rows, w_first)
    return (
        new_edge[None, None],
        aggregate[None, None],
        grad_edge[None, None],
        grad_latent[None, None],
        sums[: 3 * TILE],
        sums[3 * TILE : 4 * TILE],
        sums[4 * TILE],
    )


def solution(mesh):
    rows = P("gx", "gy", None, None)
    flat = P("gx", "gy", None)
    in_specs = (rows, rows, P(), P(), P(), rows, flat, rows, flat, flat, rows, rows)
    out_specs = (rows, rows, rows, rows, P(), P(), P())
    return jax.shard_map(
        per_device, mesh=mesh, in_specs=in_specs, out_specs=out_specs, check_vma=False
    )
```
